256 devices in a mesh: row: 8 (over z), col: 32 (over y, x, core).
Axes of the slice: x: 4, y: 4, z: 8, core: 2. Of those that a mesh axis runs over, the one named last changes fastest.
Arguments:
- right_side: float32 [4, 8192, 256], P(None, ('row', 'col')), may hold values from -6 to 6
- diag_blocks: bfloat16 [4, 4, 8192, 256], P(None, None, ('row', 'col')), may hold values from -1.2 to 4, as said below
- lower_blocks: bfloat16 [4, 4, 8192, 256], P(None, None, ('row', 'col')), may hold values from -2.390625 to 2.390625
- upper_blocks: bfloat16 [4, 4, 8192, 256], P(None, None, ('row', 'col')), may hold values from -2.390625 to 2.390625
- precond: bfloat16 [4, 4, 8192, 256], P(None, None, ('row', 'col')), may hold values from -0.2 to 0.5, as said below
- junction_out: float32 [2, 4, 4, 8192], P(None, None, None, ('row', 'col')), may hold values from -3 to 3
- junction_in: float32 [2, 4, 4, 8192], P(None, None, None, ('row', 'col')), may hold values from -3 to 3
- end_junction: int32 [2, 8192], P(None, ('row', 'col')), may hold values from 0 to 1023, as said below
- pipe_length: int32 [8192], P(('row', 'col')), may hold values from 1 to 256, 1310720 in all
Outputs:
- adjoint: float32 [4, 8192, 256], P(None, ('row', 'col'))
The draws below stay inside these ranges and needn't reach their ends.
Inputs may be any that keep to these rules, and one draw needn't show every extreme that they name: The owner column end_junction // 32 lies within 2 columns of the pipe's own mesh column, counted cyclically over the row's columns, and distance 2 occurs on both sides. `diag_blocks`: diagonally dominant: diagonal entries 2 to 4, others at most 1.2 in magnitude. `precond`: diagonal entries 0.2 to 0.5, others at most 0.2 in magnitude.
All inputs are finite; a program needn't handle non-finite values. No bound on the sum of `pipe_length` on one device may be relied on, other than what follows from the above.
Results may differ from the reference program's by a relative error of at most 0.0003.
Values sent between devices are 32-bit elements; how exact they have to be, the bound alone decides.
A program may use at most 64 MiB of HBM per device.

```python
import math
import jax
import jax.numpy as jnp
import numpy as np
from jax import lax

PIPES_DEV = 32
SEG = 256
ITERS = 4
REACH = 2
JUNC_DEV = 32
NJ_ROW = 1024
PIPES = 8192
N_ROW = 8
N_COL = 32


def draw_diag_blocks(key, part):
    key = jax.random.fold_in(key, 11)
    first, second = jax.random.split(key)
    shape = (4, 4, PIPES, SEG)
    off_part = jnp.clip(0.3 * jax.random.normal(first, shape, jnp.float32), -1.18, 1.18)
    main_part = jax.random.uniform(second, shape, jnp.float32, 2.0, 4.0)
    unit = jnp.eye(4, dtype=jnp.float32)[:, :, None, None]
    return (unit * main_part + (1.0 - unit) * off_part).astype(jnp.bfloat16)


def draw_precond(key, part):
    key = jax.random.fold_in(key, 23)
    first, second = jax.random.split(key)
    shape = (4, 4, PIPES, SEG)
    off_part = jnp.clip(0.05 * jax.random.normal(first, shape, jnp.float32), -0.198, 0.198)
    main_part = jnp.exp(jax.random.uniform(second, shape, jnp.float32, jnp.log(0.2), jnp.log(0.5)))
    unit = jnp.eye(4, dtype=jnp.float32)[:, :, None, None]
    return (unit * main_part + (1.0 - unit) * off_part).astype(jnp.bfloat16)


def draw_end_junction(key, part):
    key = jax.random.fold_in(key, 37)
    first, second = jax.random.split(key)
    column = jnp.arange(PIPES, dtype=jnp.int32) // PIPES_DEV % N_COL
    offset = jax.random.randint(first, (2, PIPES), -REACH, REACH + 1, jnp.int32)
    offset = offset.at[0, 0].set(REACH).at[1, 0].set(-REACH)
    owner = (column[None, :] + offset) % N_COL
    local = jax.random.randint(second, (2, PIPES), 0, JUNC_DEV, jnp.int32)
    local = local.at[0, 1].set(0).at[1, 1].set(JUNC_DEV - 1)
    return (owner * JUNC_DEV + local).astype(jnp.int32)


def level_of(stream_key, dims, pieces, least, largest):
    def one(position, blocks):
        heights = jax.random.uniform(jax.random.fold_in(jax.random.fold_in(stream_key, 6), position), (blocks,), jnp.float32, least / len(pieces), largest / len(pieces))
        return jnp.repeat(jnp.exp(heights), dims[position] // blocks).reshape((-1,) + (1,) * (len(dims) - position - 1))

    gain = one(*pieces[0])
    for cut in pieces[1:]:
        gain = gain * one(*cut)
    return gain


def length_profile(amount, total, most, slope):
    weights = [(1 << 20) // math.isqrt(standing ** slope) + 1 for standing in range(2, amount + 1)]
    rest, counts = total - most - (amount - 1), [1] * (amount - 1)
    while rest > 0:
        movable = [i for i in range(amount - 1) if counts[i] < most]
        whole, budget = sum([weights[i] for i in movable]), rest
        for i in movable:
            more = min(most - counts[i], max(1, budget * weights[i] // whole), rest)
            counts[i] = counts[i] + more
            rest = rest - more
    return np.array([most] + counts)


def uneven(rng, amount, total, most, skew):
    if amount == 2:
        one = jax.random.randint(rng, (), max(1, total - most), min(most, total - 1) + 1)
        return jnp.stack([one, total - one])
    lengths = jnp.asarray(length_profile(amount, total, most, skew), jnp.int32)
    pairs = (amount - 1) // 2
    source_of, receiver = lengths[1:1 + 2 * pairs:2], lengths[2:2 + 2 * pairs:2]
    slack = jnp.minimum(source_of - 1, most - receiver)
    shifted = jax.random.randint(jax.random.fold_in(rng, 1), (pairs,), 0, 1 << 20) % (slack + 1)
    lengths = lengths.at[1:1 + 2 * pairs:2].set(source_of - shifted).at[2:2 + 2 * pairs:2].set(receiver + shifted)
    return lengths[jax.random.permutation(jax.random.fold_in(rng, 2), amount)]


def bell_draw(rng, shape, spread, most, shards=(), kind=jnp.bfloat16):
    array = spread * jax.random.normal(rng, shape, jnp.float32)
    if shards:
        array = array * level_of(rng, shape, shards, -0.22, 0.18)
    return jnp.clip(array, -most, most).astype(kind)


def setup_inputs(seed: int = 0) -> dict:
    streams_of = jax.random.split(jax.random.key(seed), 10)
    return {
        "right_side": bell_draw(streams_of[0], (4, PIPES, SEG), 1.0, 6.0, ((1, 256),), jnp.float32),
        "diag_blocks": draw_diag_blocks(jax.random.fold_in(streams_of[9], 71), 0),
        "lower_blocks": bell_draw(streams_of[2], (4, 4, PIPES, SEG), 0.4, 2.390625, ((2, 256),)),
        "upper_blocks": bell_draw(streams_of[3], (4, 4, PIPES, SEG), 0.4, 2.390625, ((2, 256),)),
        "precond": draw_precond(jax.random.fold_in(streams_of[9], 71), 0),
        "junction_out": bell_draw(streams_of[5], (2, 4, 4, PIPES), 0.5, 3.0, ((3, 256),), jnp.float32),
        "junction_in": bell_draw(streams_of[6], (2, 4, 4, PIPES), 0.5, 3.0, ((3, 256),), jnp.float32),
        "end_junction": draw_end_junction(jax.random.fold_in(streams_of[9], 71), 0),
        "pipe_length": uneven(streams_of[8], PIPES, PIPES * SEG * 5 // 8, SEG, 2).astype(jnp.int32),
    }


def block_transpose(blocks, vec):
    out = blocks[0].astype(jnp.float32) * vec[0]
    for index in range(1, 4):
        out = out + blocks[index].astype(jnp.float32) * vec[index]
    return out

def block_apply(blocks, vec):
    out = blocks[:, 0].astype(jnp.float32) * vec[0]
    for index in range(1, 4):
        out = out + blocks[:, index].astype(jnp.float32) * vec[index]
    return out

def per_group(piece_fn, blocks, vec):
    groups = PIPES // PIPES_DEV

    def one_group(group):
        start = (group * PIPES_DEV).astype(jnp.int32)
        parts = tuple((lax.dynamic_slice_in_dim(b, start, PIPES_DEV, 2) for b in blocks))
        return piece_fn(parts, lax.dynamic_slice_in_dim(vec, start, PIPES_DEV, 1))
    out = lax.map(one_group, jnp.arange(groups, dtype=jnp.int32))
    return jnp.moveaxis(out, 0, 1).reshape(4, PIPES, SEG)

def pipe_part(parts, vec):
    diag_part = block_transpose(parts[0], vec)
    lower = block_transpose(parts[1], vec)
    upper = block_transpose(parts[2], vec)
    zeros = jnp.zeros_like(lower[:, :, :1])
    following = jnp.concatenate([lower[:, :, 1:], zeros], axis=2)
    preceding = jnp.concatenate([zeros, upper[:, :, :-1]], axis=2)
    return diag_part + following + preceding

def precond_part(parts, vec):
    return block_apply(parts[0], vec)

def reference(right_side, diag_blocks, lower_blocks, upper_blocks, precond, junction_out, junction_in, end_junction, pipe_length):
    slots = jnp.arange(SEG, dtype=jnp.int32)
    active = (slots[None, :] < pipe_length[:, None]).astype(jnp.float32)
    last_slot = (pipe_length - 1).astype(jnp.int32)
    pipe_row = jnp.arange(PIPES, dtype=jnp.int32) // PIPES_DEV // N_COL
    global_junction = (pipe_row[None, :] * NJ_ROW + end_junction).astype(jnp.int32)

    def operator(vec):
        body_terms = per_group(pipe_part, (diag_blocks, lower_blocks, upper_blocks), vec)
        first = vec[:, :, 0]
        last = jnp.take_along_axis(vec, last_slot[None, :, None], axis=2)[:, :, 0]
        ends = jnp.stack([first, last])
        contrib = lax.optimization_barrier(jnp.sum(junction_out * ends[:, :, None, :], axis=1))
        flat = jnp.transpose(contrib, (1, 0, 2)).reshape(4, 2 * PIPES)
        sums = jnp.zeros((4, N_ROW * NJ_ROW), jnp.float32).at[:, global_junction.reshape(-1)].add(flat)
        back = jnp.transpose(sums[:, global_junction], (1, 0, 2))
        added = lax.optimization_barrier(jnp.sum(junction_in * back[:, :, None, :], axis=1))
        at_first = jnp.where(slots[None, None, :] == 0, added[0][:, :, None], 0.0)
        at_last = jnp.where(slots[None, None, :] == last_slot[None, :, None], added[1][:, :, None], 0.0)
        return active[None] * (body_terms + at_first + at_last)

    def precondition(vec):
        return per_group(precond_part, (precond,), vec)
    start = active[None] * right_side
    beta = jnp.sqrt(jnp.sum(start * start))
    basis = [start / beta]
    hess = [[jnp.float32(0.0) for col in range(ITERS)] for rowi in range(ITERS + 1)]
    for step in range(ITERS):
        work = operator(precondition(basis[step]))
        dots = [jnp.sum(basis[i] * work) for i in range(step + 1)]
        for i in range(step + 1):
            work = work - dots[i] * basis[i]
            hess[i][step] = dots[i]
        size = jnp.sqrt(jnp.sum(work * work))
        hess[step + 1][step] = size
        basis.append(work / size)
    coeffs = least_squares(hess, beta)
    combined = coeffs[0] * basis[0]
    for step in range(1, ITERS):
        combined = combined + coeffs[step] * basis[step]
    return precondition(combined)

def least_squares(hess, beta):
    upper = [list(line) for line in hess]
    target = [beta] + [jnp.float32(0.0) * beta for i in range(ITERS)]
    cosines = []
    sines = []
    for k in range(ITERS):
        for i in range(k):
            temp = cosines[i] * upper[i][k] + sines[i] * upper[i + 1][k]
            upper[i + 1][k] = -sines[i] * upper[i][k] + cosines[i] * upper[i + 1][k]
            upper[i][k] = temp
        radius = jnp.sqrt(upper[k][k] * upper[k][k] + upper[k + 1][k] * upper[k + 1][k])
        cosines.append(upper[k][k] / radius)
        sines.append(upper[k + 1][k] / radius)
        upper[k][k] = radius
        target[k + 1] = -sines[k] * target[k]
        target[k] = cosines[k] * target[k]
    coeffs = [None] * ITERS
    for k in range(ITERS - 1, -1, -1):
        total = target[k]
        for j in range(k + 1, ITERS):
            total = total - upper[k][j] * coeffs[j]
        coeffs[k] = total / upper[k][k]
    return coeffs
```

```python
import functools

import jax
import jax.numpy as jnp
from jax import lax
from jax.experimental import pallas as pl
from jax.experimental.pallas import tpu as pltpu
from jax.sharding import PartitionSpec as P

ITERS = 4
REACH = 2
SPAN = 2 * REACH
PIECES = 2 * SPAN + 1
SHIFT = 1.0
CHUNK = 16
MESH = pl.DeviceIdType.MESH
F32 = jnp.float32
BF16 = jnp.bfloat16


def iota(shape, dim):
    return lax.broadcasted_iota(jnp.int32, shape, dim)


def split3(value):
    high = value.astype(BF16)
    rest = value - high.astype(F32)
    middle = rest.astype(BF16)
    low = (rest - middle.astype(F32)).astype(BF16)
    return high, middle, low


def dot(a, b):
    return lax.dot_general(a, b, (((1,), (0,)), ((), ())), preferred_element_type=F32)


def end_row(first, last):
    empty = jnp.zeros_like(first)
    return jnp.concatenate([first, empty, last, empty], axis=1)


def least_squares(hess, beta, steps):
    upper = [list(line) for line in hess]
    target = [beta] + [None] * steps
    cosines = []
    sines = []
    for k in range(steps):
        for i in range(k):
            temp = cosines[i] * upper[i][k] + sines[i] * upper[i + 1][k]
            upper[i + 1][k] = -sines[i] * upper[i][k] + cosines[i] * upper[i + 1][k]
            upper[i][k] = temp
        inverse = 1.0 / jnp.sqrt(upper[k][k] * upper[k][k] + upper[k + 1][k] * upper[k + 1][k])
        cosines.append(upper[k][k] * inverse)
        sines.append(upper[k + 1][k] * inverse)
        upper[k][k] = cosines[k] * upper[k][k] + sines[k] * upper[k + 1][k]
        target[k + 1] = -sines[k] * target[k]
        target[k] = cosines[k] * target[k]
    coeffs = [None] * steps
    for k in range(steps - 1, -1, -1):
        total = target[k]
        for j in range(k + 1, steps):
            total = total - upper[k][j] * coeffs[j]
        coeffs[k] = total / upper[k][k]
    return coeffs


def krylov_coeffs(gram):
    size = ITERS + 1
    low = [[None] * size for _ in range(size)]
    for j in range(size):
        total = gram[j, j]
        for k in range(j):
            total = total - low[j][k] * low[j][k]
        total = jnp.maximum(total, 1e-7 * gram[j, j])
        inverse = lax.rsqrt(total)
        low[j][j] = total * inverse
        for i in range(j + 1, size):
            total = gram[j, i]
            for k in range(j):
                total = total - low[i][k] * low[j][k]
            low[i][j] = total * inverse
    hess = [[None] * ITERS for _ in range(size)]
    for k in range(ITERS):
        for i in range(k + 2):
            hess[i][k] = low[k + 1][i]
            if i <= k:
                hess[i][k] = hess[i][k] + SHIFT * low[k][i]
    return least_squares(hess, low[0][0], ITERS)


PAIRS = [(i, j) for j in range(ITERS + 1) for i in range(j + 1)]
GRAM_ROWS = 16


def kernel(
    rows,
    columns,
    right_hbm,
    diag_hbm,
    lower_hbm,
    upper_hbm,
    precond_hbm,
    out_hbm_blocks,
    in_hbm_blocks,
    junction_hbm,
    length_hbm,
    result_hbm,
    right,
    diag,
    lower,
    upper,
    precond,
    jout,
    jin,
    junction,
    length,
    basis,
    image,
    bulk,
    result,
    sends,
    recvs,
    gram_own,
    gram_one,
    gram_two,
    in_sems,
    out_sems,
    near_send,
    near_recv,
    one_send,
    one_recv,
    two_send,
    two_recv,
):
    row = lax.axis_index("row")
    col = lax.axis_index("col")
    count_one = 2 * rows
    count_two = columns // 2
    core = col % 2
    place = col // 2
    mine_one = row * 2 + core
    mine_two = place

    def near(offset):
        return (row, (col + offset + columns) % columns)

    def member_one(step):
        index = (mine_one + step) % count_one
        return (index // 2, place * 2 + index % 2)

    def member_two(step):
        index = (mine_two + step) % count_two
        return (row, index * 2 + core)

    loads = [
        pltpu.make_async_copy(source, target, in_sems.at[index])
        for index, (source, target) in enumerate(
            [
                (length_hbm, length),
                (junction_hbm, junction),
                (out_hbm_blocks, jout),
                (in_hbm_blocks, jin),
                (right_hbm, right),
                (precond_hbm, precond),
                (diag_hbm, diag),
                (lower_hbm, lower),
                (upper_hbm, upper),
            ]
        )
    ]
    for load in loads:
        load.start()

    barrier = pltpu.get_barrier_semaphore()
    partners = [near(offset) for offset in (-3, -1, 1, 3)]
    partners += [member_one(step) for step in range(1, count_one)]
    partners += [member_two(step) for step in range(1, count_two)]
    for partner in partners:
        pl.semaphore_signal(barrier, inc=1, device_id=partner, device_id_type=MESH)

    sends[...] = jnp.zeros_like(sends)
    for load in loads[:6]:
        load.wait()

    lane = iota((1, 128), 1)
    lengths = length[...]
    length_row = end_row(lengths, lengths)
    slot_row = jnp.where(
        (lane & 32) != 0, -1, end_row(jnp.zeros_like(lengths), lengths - 1)
    )
    extract = (iota((256, 128), 0) == slot_row).astype(F32).astype(BF16)
    ids = junction[...] + 1
    id_row = jnp.where((lane & 32) != 0, -1, end_row(ids[0:1], ids[1:2]))
    square = iota((128, 128), 0) == iota((128, 128), 1)
    slot_col = jnp.sum(jnp.where(square, slot_row.astype(F32), 0.0), axis=1, keepdims=True)
    id_col = jnp.sum(jnp.where(square, id_row.astype(F32), 0.0), axis=1, keepdims=True)
    insert = (iota((128, 256), 1).astype(F32) == slot_col).astype(F32)
    insert = jnp.concatenate([insert] * 3, axis=0).astype(BF16)
    length_col = jnp.sum(
        jnp.where(square[:32], length_row.astype(F32), 0.0), axis=1, keepdims=True
    )
    active = iota((32, 256), 1).astype(F32) < length_col
    single = ((length_row == 1) & ((lane & 32) == 0)).astype(F32)
    own_pipe = (iota((32, 128), 0) == (iota((32, 128), 1) & 63))[None]

    def ends_of(value):
        total = sum(dot(part, extract) for part in split3(value.reshape(128, 256)))
        return jnp.sum(jnp.where(own_pipe, total.reshape(4, 32, 128), 0.0), axis=1)

    def at_ends(value):
        spread = jnp.where(own_pipe, value[:, None, :], 0.0).reshape(128, 128)
        return dot(jnp.concatenate(split3(spread), axis=1), insert).reshape(4, 32, 256)

    def block_row(ref, a):
        return end_row(ref[0, a], ref[1, a])

    def apply(blocks, value):
        total = blocks[0] * value[0:1]
        for a in range(1, 4):
            total = total + blocks[a] * value[a : a + 1]
        return total

    out_blocks = [block_row(jout, a) for a in range(4)]
    in_blocks = [block_row(jin, a) for a in range(4)]
    pre_ends = dot(precond[...].reshape(512, 256), extract).reshape(16, 32, 128)
    pre_ends = jnp.sum(jnp.where(own_pipe, pre_ends, 0.0), axis=1)
    to_balance = [
        sum(out_blocks[a] * pre_ends[a * 4 + b : a * 4 + b + 1] for a in range(4)) for b in range(4)
    ]

    start = jnp.where(active[None], right[...], 0.0)
    basis[0] = start
    end_values = [ends_of(start)]

    def post(step, balance):
        sends[step, 0, 0:4] = balance
        sends[step, 1, 0:4] = pltpu.roll(balance, 32, 1)
        copies = []
        for index, offset in enumerate(o for o in range(-SPAN, SPAN + 1) if o != 0):
            copy = pltpu.make_async_remote_copy(
                src_ref=sends.at[step, offset % 2],
                dst_ref=recvs.at[step, SPAN - offset],
                send_sem=near_send.at[step, index],
                recv_sem=near_recv.at[step, index],
                device_id=near(offset),
                device_id_type=MESH,
            )
            copy.start()
            copies.append(copy)
        recvs[step, SPAN] = sends[step, 0]
        return copies

    def advance(step):
        if step == 0:
            for load in loads[6:]:
                load.wait()
        for first in range(0, 32, CHUNK):
            part = slice(first, first + CHUNK)
            vec = [basis[step, b, part] for b in range(4)]
            x = []
            for a in range(4):
                total = precond[a, 0, part].astype(F32) * vec[0]
                for b in range(1, 4):
                    total = total + precond[a, b, part].astype(F32) * vec[b]
                image[step, a, part] = total
                x.append(total)
            keep = active[part]
            slot = iota((CHUNK, 256), 1)
            for b in range(4):
                sums = []
                for blocks in (diag, lower, upper):
                    total = blocks[0, b, part].astype(F32) * x[0]
                    for a in range(1, 4):
                        total = total + blocks[a, b, part].astype(F32) * x[a]
                    sums.append(total)
                following = jnp.where(slot == 255, 0.0, pltpu.roll(sums[1], 255, 1))
                preceding = jnp.where(slot == 0, 0.0, pltpu.roll(sums[2], 1, 1))
                total = jnp.where(keep, sums[0] + following + preceding, 0.0)
                bulk[b, part] = total - SHIFT * vec[b]

    def inner(left, right_part):
        total = jnp.sum(left * right_part, axis=(0, 1)).reshape(1, 256)
        return total[:, :128] + total[:, 128:]

    balance = apply(to_balance, end_values[0])
    sends[0, 0, 4:5] = jnp.maximum(id_row, 0).astype(F32)
    sends[0, 1, 4:5] = pltpu.roll(jnp.maximum(id_row, 0).astype(F32), 32, 1)
    pl.semaphore_wait(barrier, len(partners))

    pending = []
    matches = None
    for step in range(ITERS):
        copies = post(step, balance)
        pending += copies
        advance(step)
        bulk_ends = ends_of(bulk[...])
        if step == ITERS - 1:
            for index, (i, j) in enumerate(PAIRS):
                other = bulk[...] if j == ITERS else basis[j]
                value = bulk[...] if i == ITERS else basis[i]
                gram_own[0, index : index + 1] = inner(value, other)
            gram_own[0, len(PAIRS) : GRAM_ROWS] = jnp.zeros((GRAM_ROWS - len(PAIRS), 128), F32)
        for copy in copies:
            copy.wait_recv()
        joined = jnp.concatenate(
            [
                recvs[step, index] + recvs[step, index + 1]
                if index + 1 < PIECES
                else recvs[step, index]
                for index in range(0, PIECES, 2)
            ],
            axis=1,
        )
        if step == 0:
            matches = (id_col == joined[4:5]).astype(F32).T.astype(BF16)
        high = joined.astype(BF16).astype(F32)
        middle = (joined - high).astype(BF16).astype(F32)
        left = jnp.concatenate([high, middle, joined - high - middle, jnp.zeros_like(high)], axis=0)
        sums = dot(left.astype(BF16), matches)
        sums = sums[0:4] + sums[8:12] + sums[16:20]
        added = apply(in_blocks, sums)
        both = added + single * pltpu.roll(added, 64, 1)
        if step < ITERS - 1:
            end_values.append(bulk_ends + both)
            balance = apply(to_balance, end_values[-1])
            basis[step + 1] = bulk[...] + at_ends(added)
        else:
            for index, (i, j) in enumerate(PAIRS):
                if j == ITERS:
                    weight = 2.0 * bulk_ends + both if i == ITERS else end_values[i]
                    row_sum = jnp.sum(weight * added, axis=0, keepdims=True)
                    gram_own[0, index : index + 1] = gram_own[0, index : index + 1] + row_sum

    def all_sum(own, box, mine, member, count, send, recv):
        copies = []
        for step in range(1, count):
            copy = pltpu.make_async_remote_copy(
                src_ref=own,
                dst_ref=box.at[mine],
                send_sem=send.at[step],
                recv_sem=recv.at[step],
                device_id=member(step),
                device_id_type=MESH,
            )
            copy.start()
            copies.append(copy)
        box[mine] = own[...]
        for copy in copies:
            copy.wait_recv()
        return copies, jnp.sum(box[...], axis=0)

    copies, total = all_sum(
        gram_own.at[0], gram_one, mine_one, member_one, count_one, one_send, one_recv
    )
    pending += copies
    gram_own[1] = total
    copies, total = all_sum(
        gram_own.at[1], gram_two, mine_two, member_two, count_two, two_send, two_recv
    )
    pending += copies
    total = jnp.sum(total, axis=1, keepdims=True)
    gram = {pair: total[index : index + 1] for index, pair in enumerate(PAIRS)}
    coeffs = krylov_coeffs(gram)
    stores = []
    for a in range(4):
        value = coeffs[0] * image[0, a]
        for k in range(1, ITERS):
            value = value + coeffs[k] * image[k, a]
        result[a] = value
        store = pltpu.make_async_copy(result.at[a], result_hbm.at[a], out_sems.at[a])
        store.start()
        stores.append(store)
    for store in stores:
        store.wait()
    for copy in pending:
        copy.wait_send()


def body(rows, columns, right_side, diag, lower, upper, precond, jout, jin, junction, length):
    pipes, slots = right_side.shape[1:]
    length = length.reshape(1, pipes)
    operands = (right_side, diag, lower, upper, precond, jout, jin, junction, length)
    inputs = [pltpu.VMEM(value.shape, value.dtype) for value in operands]
    count_one, count_two = 2 * rows, columns // 2
    near_count = PIECES - 1
    return pl.pallas_call(
        functools.partial(kernel, rows, columns),
        out_shape=jax.ShapeDtypeStruct(right_side.shape, F32),
        in_specs=[pl.BlockSpec(memory_space=pl.ANY)] * len(operands),
        out_specs=pl.BlockSpec(memory_space=pl.ANY),
        scratch_shapes=inputs
        + [
            pltpu.VMEM((ITERS, 4, pipes, slots), F32),
            pltpu.VMEM((ITERS, 4, pipes, slots), F32),
            pltpu.VMEM((4, pipes, slots), F32),
            pltpu.VMEM((4, pipes, slots), F32),
            pltpu.VMEM((ITERS, 2, 8, 128), F32),
            pltpu.VMEM((ITERS, PIECES, 8, 128), F32),
            pltpu.VMEM((2, GRAM_ROWS, 128), F32),
            pltpu.VMEM((count_one, GRAM_ROWS, 128), F32),
            pltpu.VMEM((count_two, GRAM_ROWS, 128), F32),
            pltpu.SemaphoreType.DMA((len(operands),)),
            pltpu.SemaphoreType.DMA((4,)),
            pltpu.SemaphoreType.DMA((ITERS, near_count)),
            pltpu.SemaphoreType.DMA((ITERS, near_count)),
            pltpu.SemaphoreType.DMA((count_one,)),
            pltpu.SemaphoreType.DMA((count_one,)),
            pltpu.SemaphoreType.DMA((count_two,)),
            pltpu.SemaphoreType.DMA((count_two,)),
        ],
        compiler_params=pltpu.CompilerParams(
            collective_id=0, has_side_effects=True, vmem_limit_bytes=32 * 1024 * 1024
        ),
    )(*operands)


def solution(mesh):
    in_specs = (
        P(None, ("row", "col"), None),
        P(None, None, ("row", "col"), None),
        P(None, None, ("row", "col"), None),
        P(None, None, ("row", "col"), None),
        P(None, None, ("row", "col"), None),
        P(None, None, None, ("row", "col")),
        P(None, None, None, ("row", "col")),
        P(None, ("row", "col")),
        P(("row", "col")),
    )
    out_specs = P(None, ("row", "col"), None)
    run = functools.partial(body, mesh.shape["row"], mesh.shape["col"])
    return jax.shard_map(run, mesh=mesh, in_specs=in_specs, out_specs=out_specs, check_vma=False)
```

```python
import functools

import jax
import jax.numpy as jnp
from jax import lax
from jax.experimental import pallas as pl
from jax.experimental.pallas import tpu as pltpu
from jax.sharding import PartitionSpec as P

ITERS = 4
REACH = 2
SPAN = 2 * REACH
PIECES = 2 * SPAN + 1
SHIFT = 1.0
CHUNK = 16
MESH = pl.DeviceIdType.MESH
F32 = jnp.float32
BF16 = jnp.bfloat16


def iota(shape, dim):
    return lax.broadcasted_iota(jnp.int32, shape, dim)


def split3(value):
    high = value.astype(BF16)
    rest = value - high.astype(F32)
    middle = rest.astype(BF16)
    low = (rest - middle.astype(F32)).astype(BF16)
    return high, middle, low


def dot(a, b):
    return lax.dot_general(a, b, (((1,), (0,)), ((), ())), preferred_element_type=F32)


def end_row(first, last):
    empty = jnp.zeros_like(first)
    return jnp.concatenate([first, empty, last, empty], axis=1)


def least_squares(hess, beta, steps):
    upper = [list(line) for line in hess]
    target = [beta] + [None] * steps
    cosines = []
    sines = []
    for k in range(steps):
        for i in range(k):
            temp = cosines[i] * upper[i][k] + sines[i] * upper[i + 1][k]
            upper[i + 1][k] = -sines[i] * upper[i][k] + cosines[i] * upper[i + 1][k]
            upper[i][k] = temp
        inverse = 1.0 / jnp.sqrt(upper[k][k] * upper[k][k] + upper[k + 1][k] * upper[k + 1][k])
        cosines.append(upper[k][k] * inverse)
        sines.append(upper[k + 1][k] * inverse)
        upper[k][k] = cosines[k] * upper[k][k] + sines[k] * upper[k + 1][k]
        target[k + 1] = -sines[k] * target[k]
        target[k] = cosines[k] * target[k]
    coeffs = [None] * steps
    for k in range(steps - 1, -1, -1):
        total = target[k]
        for j in range(k + 1, steps):
            total = total - upper[k][j] * coeffs[j]
        coeffs[k] = total / upper[k][k]
    return coeffs


def krylov_coeffs(gram):
    size = ITERS + 1
    low = [[None] * size for _ in range(size)]
    for j in range(size):
        total = gram[j, j]
        for k in range(j):
            total = total - low[j][k] * low[j][k]
        total = jnp.maximum(total, 1e-7 * gram[j, j])
        inverse = lax.rsqrt(total)
        low[j][j] = total * inverse
        for i in range(j + 1, size):
            total = gram[j, i]
            for k in range(j):
                total = total - low[i][k] * low[j][k]
            low[i][j] = total * inverse
    hess = [[None] * ITERS for _ in range(size)]
    for k in range(ITERS):
        for i in range(k + 2):
            hess[i][k] = low[k + 1][i]
            if i <= k:
                hess[i][k] = hess[i][k] + SHIFT * low[k][i]
    return least_squares(hess, low[0][0], ITERS)


PAIRS = [(i, j) for j in range(ITERS + 1) for i in range(j + 1)]
GRAM_ROWS = 16


def kernel(
    rows,
    columns,
    right_hbm,
    diag_hbm,
    lower_hbm,
    upper_hbm,
    precond_hbm,
    out_hbm_blocks,
    in_hbm_blocks,
    junction_hbm,
    length_hbm,
    result_hbm,
    right,
    diag,
    lower,
    upper,
    precond,
    jout,
    jin,
    junction,
    length,
    basis,
    image,
    bulk,
    result,
    sends,
    recvs,
    gram_own,
    gram_one,
    gram_two,
    in_sems,
    out_sems,
    near_send,
    near_recv,
    one_send,
    one_recv,
    two_send,
    two_recv,
):
    row = lax.axis_index("row")
    col = lax.axis_index("col")
    count_one = 2 * rows
    count_two = columns // 2
    core = col % 2
    place = col // 2
    mine_one = row * 2 + core
    mine_two = place

    def near(offset):
        return (row, (col + offset + columns) % columns)

    def member_one(step):
        index = (mine_one + step) % count_one
        return (index // 2, place * 2 + index % 2)

    def member_two(step):
        index = (mine_two + step) % count_two
        return (row, index * 2 + core)

    loads = [
        pltpu.make_async_copy(source, target, in_sems.at[index])
        for index, (source, target) in enumerate(
            [
                (length_hbm, length),
                (junction_hbm, junction),
                (out_hbm_blocks, jout),
                (in_hbm_blocks, jin),
                (right_hbm, right),
                (precond_hbm, precond),
                (diag_hbm, diag),
                (lower_hbm, lower),
                (upper_hbm, upper),
            ]
        )
    ]
    for load in loads:
        load.start()

    barrier = pltpu.get_barrier_semaphore()
    partners = [near(offset) for offset in (-3, -1, 1, 3)]
    partners += [member_one(step) for step in range(1, count_one)]
    partners += [member_two(step) for step in range(1, count_two)]
    for partner in partners:
        pl.semaphore_signal(barrier, inc=1, device_id=partner, device_id_type=MESH)

    sends[...] = jnp.zeros_like(sends)
    for load in loads[:6]:
        load.wait()

    lane = iota((1, 128), 1)
    lengths = length[...]
    length_row = end_row(lengths, lengths)
    slot_row = jnp.where(
        (lane & 32) != 0, -1, end_row(jnp.zeros_like(lengths), lengths - 1)
    )
    extract = (iota((256, 128), 0) == slot_row).astype(F32).astype(BF16)
    ids = junction[...] + 1
    id_row = jnp.where((lane & 32) != 0, -1, end_row(ids[0:1], ids[1:2]))
    square = iota((128, 128), 0) == iota((128, 128), 1)
    slot_col = jnp.sum(jnp.where(square, slot_row.astype(F32), 0.0), axis=1, keepdims=True)
    id_col = jnp.sum(jnp.where(square, id_row.astype(F32), 0.0), axis=1, keepdims=True)
    insert = (iota((128, 256), 1).astype(F32) == slot_col).astype(F32)
    insert = jnp.concatenate([insert] * 3, axis=0).astype(BF16)
    length_col = jnp.sum(
        jnp.where(square[:32], length_row.astype(F32), 0.0), axis=1, keepdims=True
    )
    active = iota((32, 256), 1).astype(F32) < length_col
    single = ((length_row == 1) & ((lane & 32) == 0)).astype(F32)
    own_pipe = (iota((32, 128), 0) == (iota((32, 128), 1) & 63))[None]

    def ends_of(value):
        total = sum(dot(part, extract) for part in split3(value.reshape(128, 256)))
        return jnp.sum(jnp.where(own_pipe, total.reshape(4, 32, 128), 0.0), axis=1)

    def at_ends(value):
        spread = jnp.where(own_pipe, value[:, None, :], 0.0).reshape(128, 128)
        return dot(jnp.concatenate(split3(spread), axis=1), insert).reshape(4, 32, 256)

    def block_row(ref, a):
        return end_row(ref[0, a], ref[1, a])

    def apply(blocks, value):
        total = blocks[0] * value[0:1]
        for a in range(1, 4):
            total = total + blocks[a] * value[a : a + 1]
        return total

    out_blocks = [block_row(jout, a) for a in range(4)]
    in_blocks = [block_row(jin, a) for a in range(4)]
    pre_ends = dot(precond[...].reshape(512, 256), extract).reshape(16, 32, 128)
    pre_ends = jnp.sum(jnp.where(own_pipe, pre_ends, 0.0), axis=1)
    to_balance = [
        sum(out_blocks[a] * pre_ends[a * 4 + b : a * 4 + b + 1] for a in range(4)) for b in range(4)
    ]

    start = jnp.where(active[None], right[...], 0.0)
    basis[0] = start
    end_values = [ends_of(start)]

    def post(step, balance):
        sends[step, 0, 0:4] = balance
        sends[step, 1, 0:4] = pltpu.roll(balance, 32, 1)
        copies = []
        for index, offset in enumerate(o for o in range(-SPAN, SPAN + 1) if o != 0):
            copy = pltpu.make_async_remote_copy(
                src_ref=sends.at[step, offset % 2],
                dst_ref=recvs.at[step, SPAN - offset],
                send_sem=near_send.at[step, index],
                recv_sem=near_recv.at[step, index],
                device_id=near(offset),
                device_id_type=MESH,
            )
            copy.start()
            copies.append(copy)
        recvs[step, SPAN] = sends[step, 0]
        return copies

    def advance(step):
        if step == 0:
            for load in loads[6:]:
                load.wait()
        for first in range(0, 32, CHUNK):
            part = slice(first, first + CHUNK)
            vec = [basis[step, b, part] for b in range(4)]
            x = []
            for a in range(4):
                total = precond[a, 0, part].astype(F32) * vec[0]
                for b in range(1, 4):
                    total = total + precond[a, b, part].astype(F32) * vec[b]
                image[step, a, part] = total
                x.append(total)
            keep = active[part]
            slot = iota((CHUNK, 256), 1)
            for b in range(4):
                sums = []
                for blocks in (diag, lower, upper):
                    total = blocks[0, b, part].astype(F32) * x[0]
                    for a in range(1, 4):
                        total = total + blocks[a, b, part].astype(F32) * x[a]
                    sums.append(total)
                following = jnp.where(slot == 255, 0.0, pltpu.roll(sums[1], 255, 1))
                preceding = jnp.where(slot == 0, 0.0, pltpu.roll(sums[2], 1, 1))
                total = jnp.where(keep, sums[0] + following + preceding, 0.0)
                bulk[b, part] = total - SHIFT * vec[b]

    def inner(left, right_part):
        total = jnp.sum(left * right_part, axis=(0, 1)).reshape(1, 256)
        return total[:, :128] + total[:, 128:]

    balance = apply(to_balance, end_values[0])
    sends[0, 0, 4:5] = jnp.maximum(id_row, 0).astype(F32)
    sends[0, 1, 4:5] = pltpu.roll(jnp.maximum(id_row, 0).astype(F32), 32, 1)
    pl.semaphore_wait(barrier, len(partners))

    pending = []
    matches = None
    for step in range(ITERS):
        copies = post(step, balance)
        pending += copies
        advance(step)
        bulk_ends = ends_of(bulk[...])
        if step == ITERS - 1:
            for index, (i, j) in enumerate(PAIRS):
                other = bulk[...] if j == ITERS else basis[j]
                value = bulk[...] if i == ITERS else basis[i]
                gram_own[0, index : index + 1] = inner(value, other)
            gram_own[0, len(PAIRS) : GRAM_ROWS] = jnp.zeros((GRAM_ROWS - len(PAIRS), 128), F32)
        for copy in copies:
            copy.wait_recv()
        joined = jnp.concatenate(
            [
                recvs[step, index] + recvs[step, index + 1]
                if index + 1 < PIECES
                else recvs[step, index]
                for index in range(0, PIECES, 2)
            ],
            axis=1,
        )
        if step == 0:
            matches = (id_col == joined[4:5]).astype(F32).T.astype(BF16)
        high = joined.astype(BF16).astype(F32)
        middle = (joined - high).astype(BF16).astype(F32)
        left = jnp.concatenate([high, middle, joined - high - middle, jnp.zeros_like(high)], axis=0)
        sums = dot(left.astype(BF16), matches)
        sums = sums[0:4] + sums[8:12] + sums[16:20]
        added = apply(in_blocks, sums)
        both = added + single * pltpu.roll(added, 64, 1)
        if step < ITERS - 1:
            end_values.append(bulk_ends + both)
            balance = apply(to_balance, end_values[-1])
            basis[step + 1] = bulk[...] + at_ends(added)
        else:
            for index, (i, j) in enumerate(PAIRS):
                if j == ITERS:
                    weight = 2.0 * bulk_ends + both if i == ITERS else end_values[i]
                    row_sum = jnp.sum(weight * added, axis=0, keepdims=True)
                    gram_own[0, index : index + 1] = gram_own[0, index : index + 1] + row_sum

    def all_sum(own, box, mine, member, count, send, recv):
        copies = []
        for step in range(1, count):
            copy = pltpu.make_async_remote_copy(
                src_ref=own,
                dst_ref=box.at[mine],
                send_sem=send.at[step],
                recv_sem=recv.at[step],
                device_id=member(step),
                device_id_type=MESH,
            )
            copy.start()
            copies.append(copy)
        box[mine] = own[...]
        for copy in copies:
            copy.wait_recv()
        return copies, jnp.sum(box[...], axis=0)

    partial = jnp.sum(gram_own[0], axis=1, keepdims=True)
    eye = iota((GRAM_ROWS, 128), 0) == iota((GRAM_ROWS, 128), 1)
    gram_own[1, 0:1] = jnp.sum(jnp.where(eye, partial, 0.0), axis=0, keepdims=True)
    copies, total = all_sum(
        gram_own.at[1, 0:1], gram_one, mine_one, member_one, count_one, one_send, one_recv
    )
    pending += copies
    gram_own[1, 8:9] = total
    copies, total = all_sum(
        gram_own.at[1, 8:9], gram_two, mine_two, member_two, count_two, two_send, two_recv
    )
    pending += copies
    gram = {pair: total[:, index : index + 1] for index, pair in enumerate(PAIRS)}
    coeffs = krylov_coeffs(gram)
    stores = []
    for a in range(4):
        value = coeffs[0] * image[0, a]
        for k in range(1, ITERS):
            value = value + coeffs[k] * image[k, a]
        result[a] = value
        store = pltpu.make_async_copy(result.at[a], result_hbm.at[a], out_sems.at[a])
        store.start()
        stores.append(store)
    for store in stores:
        store.wait()
    for copy in pending:
        copy.wait_send()


def body(rows, columns, right_side, diag, lower, upper, precond, jout, jin, junction, length):
    pipes, slots = right_side.shape[1:]
    length = length.reshape(1, pipes)
    operands = (right_side, diag, lower, upper, precond, jout, jin, junction, length)
    inputs = [pltpu.VMEM(value.shape, value.dtype) for value in operands]
    count_one, count_two = 2 * rows, columns // 2
    near_count = PIECES - 1
    return pl.pallas_call(
        functools.partial(kernel, rows, columns),
        out_shape=jax.ShapeDtypeStruct(right_side.shape, F32),
        in_specs=[pl.BlockSpec(memory_space=pl.ANY)] * len(operands),
        out_specs=pl.BlockSpec(memory_space=pl.ANY),
        scratch_shapes=inputs
        + [
            pltpu.VMEM((ITERS, 4, pipes, slots), F32),
            pltpu.VMEM((ITERS, 4, pipes, slots), F32),
            pltpu.VMEM((4, pipes, slots), F32),
            pltpu.VMEM((4, pipes, slots), F32),
            pltpu.VMEM((ITERS, 2, 8, 128), F32),
            pltpu.VMEM((ITERS, PIECES, 8, 128), F32),
            pltpu.VMEM((2, GRAM_ROWS, 128), F32),
            pltpu.VMEM((count_one, 1, 128), F32),
            pltpu.VMEM((count_two, 1, 128), F32),
            pltpu.SemaphoreType.DMA((len(operands),)),
            pltpu.SemaphoreType.DMA((4,)),
            pltpu.SemaphoreType.DMA((ITERS, near_count)),
            pltpu.SemaphoreType.DMA((ITERS, near_count)),
            pltpu.SemaphoreType.DMA((count_one,)),
            pltpu.SemaphoreType.DMA((count_one,)),
            pltpu.SemaphoreType.DMA((count_two,)),
            pltpu.SemaphoreType.DMA((count_two,)),
        ],
        compiler_params=pltpu.CompilerParams(
            collective_id=0, has_side_effects=True, vmem_limit_bytes=63 * 1024 * 1024
        ),
    )(*operands)


def solution(mesh):
    in_specs = (
        P(None, ("row", "col"), None),
        P(None, None, ("row", "col"), None),
        P(None, None, ("row", "col"), None),
        P(None, None, ("row", "col"), None),
        P(None, None, ("row", "col"), None),
        P(None, None, None, ("row", "col")),
        P(None, None, None, ("row", "col")),
        P(None, ("row", "col")),
        P(("row", "col")),
    )
    out_specs = P(None, ("row", "col"), None)
    run = functools.partial(body, mesh.shape["row"], mesh.shape["col"])
    return jax.shard_map(run, mesh=mesh, in_specs=in_specs, out_specs=out_specs, check_vma=False)
```

```python
import functools

import jax
import jax.numpy as jnp
from jax import lax
from jax.experimental import pallas as pl
from jax.experimental.pallas import tpu as pltpu
from jax.sharding import PartitionSpec as P

ITERS = 4
REACH = 2
SPAN = 2 * REACH
FAR = 2 * SPAN
PIECES = 2 * SPAN + 1
PEERS = 2 * FAR + 1
SHIFT = 1.0
CHUNK = 16
MESH = pl.DeviceIdType.MESH
F32 = jnp.float32
BF16 = jnp.bfloat16


def iota(shape, dim):
    return lax.broadcasted_iota(jnp.int32, shape, dim)


def split3(value):
    high = value.astype(BF16)
    rest = value - high.astype(F32)
    middle = rest.astype(BF16)
    low = (rest - middle.astype(F32)).astype(BF16)
    return high, middle, low


def dot(a, b):
    return lax.dot_general(a, b, (((1,), (0,)), ((), ())), preferred_element_type=F32)


def end_row(first, last):
    empty = jnp.zeros_like(first)
    return jnp.concatenate([first, empty, last, empty], axis=1)


def least_squares(hess, beta, steps):
    upper = [list(line) for line in hess]
    target = [beta] + [None] * steps
    cosines = []
    sines = []
    for k in range(steps):
        for i in range(k):
            temp = cosines[i] * upper[i][k] + sines[i] * upper[i + 1][k]
            upper[i + 1][k] = -sines[i] * upper[i][k] + cosines[i] * upper[i + 1][k]
            upper[i][k] = temp
        inverse = 1.0 / jnp.sqrt(upper[k][k] * upper[k][k] + upper[k + 1][k] * upper[k + 1][k])
        cosines.append(upper[k][k] * inverse)
        sines.append(upper[k + 1][k] * inverse)
        upper[k][k] = cosines[k] * upper[k][k] + sines[k] * upper[k + 1][k]
        target[k + 1] = -sines[k] * target[k]
        target[k] = cosines[k] * target[k]
    coeffs = [None] * steps
    for k in range(steps - 1, -1, -1):
        total = target[k]
        for j in range(k + 1, steps):
            total = total - upper[k][j] * coeffs[j]
        coeffs[k] = total / upper[k][k]
    return coeffs


def krylov_coeffs(gram):
    size = ITERS + 1
    low = [[None] * size for _ in range(size)]
    for j in range(size):
        total = gram[j, j]
        for k in range(j):
            total = total - low[j][k] * low[j][k]
        total = jnp.maximum(total, 1e-7 * gram[j, j])
        inverse = lax.rsqrt(total)
        low[j][j] = total * inverse
        for i in range(j + 1, size):
            total = gram[j, i]
            for k in range(j):
                total = total - low[i][k] * low[j][k]
            low[i][j] = total * inverse
    hess = [[None] * ITERS for _ in range(size)]
    for k in range(ITERS):
        for i in range(k + 2):
            hess[i][k] = low[k + 1][i]
            if i <= k:
                hess[i][k] = hess[i][k] + SHIFT * low[k][i]
    return least_squares(hess, low[0][0], ITERS)


PAIRS = [(i, j) for j in range(ITERS + 1) for i in range(j + 1)]
GRAM_ROWS = 16


def kernel(
    rows,
    columns,
    right_hbm,
    diag_hbm,
    lower_hbm,
    upper_hbm,
    precond_hbm,
    out_hbm_blocks,
    in_hbm_blocks,
    junction_hbm,
    length_hbm,
    result,
    right,
    diag,
    lower,
    upper,
    precond,
    jout,
    jin,
    junction,
    length,
    basis,
    image,
    bulk,
    sends_one,
    sends_two,
    recvs_one,
    recvs_two,
    gram_own,
    gram_one,
    gram_two,
    in_sems,
    near_send,
    near_recv,
    one_send,
    one_recv,
    two_send,
    two_recv,
):
    row = lax.axis_index("row")
    col = lax.axis_index("col")
    count_one = 2 * rows
    count_two = columns // 2
    core = col % 2
    place = col // 2
    mine_one = row * 2 + core
    mine_two = place

    def near(offset):
        return (row, (col + offset + columns) % columns)

    def member_one(step):
        index = (mine_one + step) % count_one
        return (index // 2, place * 2 + index % 2)

    def member_two(step):
        index = (mine_two + step) % count_two
        return (row, index * 2 + core)

    loads = [
        pltpu.make_async_copy(source, target, in_sems.at[index])
        for index, (source, target) in enumerate(
            [
                (length_hbm, length),
                (junction_hbm, junction),
                (out_hbm_blocks, jout),
                (in_hbm_blocks, jin),
                (right_hbm, right),
                (precond_hbm, precond),
                (diag_hbm, diag),
                (lower_hbm, lower),
                (upper_hbm, upper),
            ]
        )
    ]
    for load in loads:
        load.start()

    barrier = pltpu.get_barrier_semaphore()
    partners = [near(offset) for offset in range(1 - FAR, FAR, 2)]
    partners += [member_one(step) for step in range(1, count_one)]
    partners += [member_two(step) for step in range(1, count_two)]
    for partner in partners:
        pl.semaphore_signal(barrier, inc=1, device_id=partner, device_id_type=MESH)

    sends_one[...] = jnp.zeros_like(sends_one)
    sends_two[...] = jnp.zeros_like(sends_two)
    for load in loads[:6]:
        load.wait()

    lane = iota((1, 128), 1)
    lengths = length[...]
    length_row = end_row(lengths, lengths)
    slot_row = jnp.where(
        (lane & 32) != 0, -1, end_row(jnp.zeros_like(lengths), lengths - 1)
    )
    extract = (iota((256, 128), 0) == slot_row).astype(F32).astype(BF16)
    ids = junction[...]
    owned = ids % 32
    ids = (ids // 32 - col + REACH + columns) % columns * 32 + owned
    slot_of_junction_row = jnp.where((lane & 32) != 0, -1, end_row(ids[0:1], ids[1:2])).astype(F32)
    square = iota((128, 128), 0) == iota((128, 128), 1)
    slot_col = jnp.sum(jnp.where(square, slot_row.astype(F32), 0.0), axis=1, keepdims=True)
    slot_of_junction_col = jnp.sum(
        jnp.where(square, slot_of_junction_row, 0.0), axis=1, keepdims=True
    )
    insert = (iota((128, 256), 1).astype(F32) == slot_col).astype(F32)
    insert = jnp.concatenate([insert] * 3, axis=0).astype(BF16)
    length_col = jnp.sum(
        jnp.where(square[:32], length_row.astype(F32), 0.0), axis=1, keepdims=True
    )
    active = iota((32, 256), 1).astype(F32) < length_col
    single = ((length_row == 1) & ((lane & 32) == 0)).astype(F32)
    own_pipe = (iota((32, 128), 0) == (iota((32, 128), 1) & 63))[None]

    def ends_of(value):
        total = sum(dot(part, extract) for part in split3(value.reshape(128, 256)))
        return jnp.sum(jnp.where(own_pipe, total.reshape(4, 32, 128), 0.0), axis=1)

    def at_ends(value):
        spread = jnp.where(own_pipe, value[:, None, :], 0.0).reshape(128, 128)
        return dot(jnp.concatenate(split3(spread), axis=1), insert).reshape(4, 32, 256)

    def block_row(ref, a):
        return end_row(ref[0, a], ref[1, a])

    def apply(blocks, value):
        total = blocks[0] * value[0:1]
        for a in range(1, 4):
            total = total + blocks[a] * value[a : a + 1]
        return total

    out_blocks = [block_row(jout, a) for a in range(4)]
    in_blocks = [block_row(jin, a) for a in range(4)]
    pre_ends = dot(precond[...].reshape(512, 256), extract).reshape(16, 32, 128)
    pre_ends = jnp.sum(jnp.where(own_pipe, pre_ends, 0.0), axis=1)
    to_balance = [
        sum(out_blocks[a] * pre_ends[a * 4 + b : a * 4 + b + 1] for a in range(4)) for b in range(4)
    ]

    to_table = (slot_of_junction_col == iota((128, 256), 1).astype(F32)).astype(F32).astype(BF16)

    def stacked(value):
        high = value.astype(BF16).astype(F32)
        middle = (value - high).astype(BF16).astype(F32)
        low = value - high - middle
        return jnp.concatenate([high, middle, low, jnp.zeros_like(high)], axis=0).astype(BF16)

    def unstacked(total):
        return total[0:8] + total[8:16] + total[16:24]

    def eight(value):
        return jnp.concatenate([value, jnp.zeros_like(value)], axis=0)

    def post(sends, recvs, near_rows, send_sem, recv_sem, balance, free):
        table = unstacked(dot(stacked(eight(balance)), to_table))
        for version in range(4):
            shifted = pltpu.roll(table, 32 * version, 1) if version else table
            sends[version, 0:4] = shifted[0:4, :128]
            sends[version, 4:8] = shifted[0:4, 128:]
            sends[version, 8:12] = pltpu.roll(free, 32, 1) if version % 2 else free
        copies = []
        for offset in sorted(range(-FAR, FAR + 1), key=lambda o: -abs(o)):
            if offset == 0:
                continue
            count = near_rows if abs(offset) <= SPAN else 8
            copy = pltpu.make_async_remote_copy(
                src_ref=sends.at[-offset % 4, 0:count],
                dst_ref=recvs.at[FAR - offset, 0:count],
                send_sem=send_sem.at[FAR + offset],
                recv_sem=recv_sem.at[FAR + offset],
                device_id=near(offset),
                device_id_type=MESH,
            )
            copy.start()
            copies.append(copy)
        recvs[FAR, 0:near_rows] = sends[0, 0:near_rows]
        return copies

    def pieces(recvs, part):
        joined = []
        for index in range(0, PIECES, 2):
            value = recvs[SPAN + index, part]
            if index + 1 < PIECES:
                value = value + recvs[SPAN + index + 1, part]
            joined.append(value)
        return joined

    def balances(recvs, gather, frees, blocks, crosses, matches):
        starts = []
        for first in range(0, PEERS, 4):
            total = recvs[first, 0:8]
            for index in range(first + 1, min(first + 4, PEERS)):
                total = total + recvs[index, 0:8]
            starts.append(total)
        table = [starts[k + 1] + pltpu.roll(starts[k], 4, 0) for k in range(4)]
        left = stacked(jnp.concatenate(table, axis=1))
        first = [
            unstacked(dot(left[:, 128 * (j // 2) : 128 * (j // 2) + 256], gather[j]))[0:4]
            for j in range(5)
        ]
        second = []
        for j in range(5):
            turned = pltpu.roll(first[j], 96, 1)
            cross = apply(crosses[j], turned)
            second.append(frees[j] + apply(blocks[j], first[j]) + pltpu.roll(cross, 96, 1))
        own = dot(stacked(eight(jnp.concatenate(second, axis=1))), matches)
        return first[2], unstacked(own)[0:4]

    def advance(step):
        if step == 0:
            for load in loads[6:]:
                load.wait()
        for first in range(0, 32, CHUNK):
            part = slice(first, first + CHUNK)
            vec = [basis[step, b, part] for b in range(4)]
            x = []
            for a in range(4):
                total = precond[a, 0, part].astype(F32) * vec[0]
                for b in range(1, 4):
                    total = total + precond[a, b, part].astype(F32) * vec[b]
                image[step, a, part] = total
                x.append(total)
            keep = active[part]
            slot = iota((CHUNK, 256), 1)
            for b in range(4):
                sums = []
                for blocks in (diag, lower, upper):
                    total = blocks[0, b, part].astype(F32) * x[0]
                    for a in range(1, 4):
                        total = total + blocks[a, b, part].astype(F32) * x[a]
                    sums.append(total)
                following = jnp.where(slot == 255, 0.0, pltpu.roll(sums[1], 255, 1))
                preceding = jnp.where(slot == 0, 0.0, pltpu.roll(sums[2], 1, 1))
                total = jnp.where(keep, sums[0] + following + preceding, 0.0)
                bulk[b, part] = total - SHIFT * vec[b]

    def inner(left, right_part):
        total = jnp.sum(left * right_part, axis=(0, 1)).reshape(1, 256)
        return total[:, :128] + total[:, 128:]

    def gram_rows(last, first_pair, last_pair):
        for index, (i, j) in enumerate(PAIRS[first_pair:last_pair], first_pair):
            gram_own[0, index : index + 1] = inner(last[i], last[j])

    half = (lane & 32) == 0
    pack = []
    for a in range(4):
        turned = pltpu.roll(in_blocks[a], 64, 1)
        own = apply(to_balance, in_blocks[a])
        cross = single * apply(to_balance, turned)
        pack.append(own + pltpu.roll(cross, 32, 1))
    pack = jnp.concatenate(pack, axis=0)
    place_row = jnp.where((lane & 32) == 0, slot_of_junction_row + 1.0, 0.0)
    for version in range(4):
        turn = 32 * (version % 2)
        sends_one[version, 12:13] = pltpu.roll(place_row, turn, 1) if turn else place_row
        sends_one[version, 16:32] = pltpu.roll(pack, turn, 1) if turn else pack

    start = jnp.where(active[None], right[...], 0.0)
    basis[0] = start
    balance = apply(to_balance, ends_of(start))
    advance(0)
    free = apply(to_balance, ends_of(bulk[...]))
    pl.semaphore_wait(barrier, len(partners))
    copies = post(sends_one, recvs_one, 32, near_send.at[0], near_recv.at[0], balance, free)
    pending = list(copies)
    for copy in copies:
        copy.wait_recv()

    joined = pieces(recvs_one, slice(8, 16))
    gather = []
    place_rows = []
    for j in range(5):
        tagged = joined[j][4:5]
        column = 2.0 * j + jnp.where(half, 0.0, 1.0)
        position = jnp.where(tagged > 0.5, tagged - 1.0 + 32.0 * column, -1000.0)
        place_rows.append(position)
        rows_of = iota((256, 128), 0).astype(F32) + 128.0 * (j // 2)
        gather.append((rows_of == position).astype(F32).astype(BF16))
    own_place = jnp.where(slot_of_junction_col < 0.0, -2000.0, slot_of_junction_col + 128.0)
    matches = (own_place == jnp.concatenate(place_rows, axis=1)).astype(F32).T.astype(BF16)
    blocks = []
    crosses = []
    for index in range(0, PIECES, 2):
        even = recvs_one[SPAN + index, 16:32]
        odd = recvs_one[SPAN + index + 1, 16:32] if index + 1 < PIECES else jnp.zeros_like(even)
        own = jnp.where(half, even, odd)
        cross = jnp.where(half, odd, even)
        blocks.append([own[4 * a : 4 * a + 4] for a in range(4)])
        crosses.append([cross[4 * a : 4 * a + 4] for a in range(4)])

    first, second = balances(
        recvs_one, gather, [value[0:4] for value in joined], blocks, crosses, matches
    )
    basis[1] = bulk[...] + at_ends(apply(in_blocks, first))
    advance(1)
    basis[2] = bulk[...] + at_ends(apply(in_blocks, second))
    balance = apply(to_balance, ends_of(basis[2]))
    advance(2)
    free = apply(to_balance, ends_of(bulk[...]))
    copies = post(sends_two, recvs_two, 16, near_send.at[1], near_recv.at[1], balance, free)
    pending += copies
    gram_rows(basis, 0, 6)
    gram_own[0, len(PAIRS) : GRAM_ROWS] = jnp.zeros((GRAM_ROWS - len(PAIRS), 128), F32)
    for copy in copies:
        copy.wait_recv()

    joined = pieces(recvs_two, slice(8, 16))
    first, second = balances(
        recvs_two, gather, [value[0:4] for value in joined], blocks, crosses, matches
    )
    basis[3] = bulk[...] + at_ends(apply(in_blocks, first))
    advance(3)
    basis[4] = bulk[...] + at_ends(apply(in_blocks, second))
    gram_rows(basis, 6, len(PAIRS))

    def all_sum(own, box, mine, member, count, send, recv):
        copies = []
        for step in range(1, count):
            copy = pltpu.make_async_remote_copy(
                src_ref=own,
                dst_ref=box.at[mine],
                send_sem=send.at[step],
                recv_sem=recv.at[step],
                device_id=member(step),
                device_id_type=MESH,
            )
            copy.start()
            copies.append(copy)
        box[mine] = own[...]
        for copy in copies:
            copy.wait_recv()
        return copies, jnp.sum(box[...], axis=0)

    partial = jnp.sum(gram_own[0], axis=1, keepdims=True)
    eye = iota((GRAM_ROWS, 128), 0) == iota((GRAM_ROWS, 128), 1)
    gram_own[1, 0:1] = jnp.sum(jnp.where(eye, partial, 0.0), axis=0, keepdims=True)
    copies, total = all_sum(
        gram_own.at[1, 0:1], gram_one, mine_one, member_one, count_one, one_send, one_recv
    )
    pending += copies
    gram_own[1, 8:9] = total
    copies, total = all_sum(
        gram_own.at[1, 8:9], gram_two, mine_two, member_two, count_two, two_send, two_recv
    )
    pending += copies
    gram = {pair: total[:, index : index + 1] for index, pair in enumerate(PAIRS)}
    coeffs = krylov_coeffs(gram)
    for a in range(4):
        value = coeffs[0] * image[0, a]
        for k in range(1, ITERS):
            value = value + coeffs[k] * image[k, a]
        result[a] = value
    for copy in pending:
        copy.wait_send()


def body(rows, columns, right_side, diag, lower, upper, precond, jout, jin, junction, length):
    pipes, slots = right_side.shape[1:]
    length = length.reshape(1, pipes)
    operands = (right_side, diag, lower, upper, precond, jout, jin, junction, length)
    held = [pltpu.with_memory_space_constraint(value, pltpu.HBM) for value in operands]
    inputs = [pltpu.VMEM(value.shape, value.dtype) for value in operands]
    count_one, count_two = 2 * rows, columns // 2
    return pl.pallas_call(
        functools.partial(kernel, rows, columns),
        out_shape=pltpu.VMEM(right_side.shape, F32),
        in_specs=[pl.BlockSpec(memory_space=pltpu.HBM)] * len(operands),
        out_specs=pl.BlockSpec(memory_space=pltpu.VMEM),
        scratch_shapes=inputs
        + [
            pltpu.VMEM((ITERS + 1, 4, pipes, slots), F32),
            pltpu.VMEM((ITERS, 4, pipes, slots), F32),
            pltpu.VMEM((4, pipes, slots), F32),
            pltpu.VMEM((4, 32, 128), F32),
            pltpu.VMEM((4, 16, 128), F32),
            pltpu.VMEM((PEERS, 32, 128), F32),
            pltpu.VMEM((PEERS, 16, 128), F32),
            pltpu.VMEM((2, GRAM_ROWS, 128), F32),
            pltpu.VMEM((count_one, 1, 128), F32),
            pltpu.VMEM((count_two, 1, 128), F32),
            pltpu.SemaphoreType.DMA((len(operands),)),
            pltpu.SemaphoreType.DMA((2, PEERS)),
            pltpu.SemaphoreType.DMA((2, PEERS)),
            pltpu.SemaphoreType.DMA((count_one,)),
            pltpu.SemaphoreType.DMA((count_one,)),
            pltpu.SemaphoreType.DMA((count_two,)),
            pltpu.SemaphoreType.DMA((count_two,)),
        ],
        compiler_params=pltpu.CompilerParams(
            collective_id=0, has_side_effects=True, vmem_limit_bytes=48 * 1024 * 1024
        ),
    )(*held)


def solution(mesh):
    in_specs = (
        P(None, ("row", "col"), None),
        P(None, None, ("row", "col"), None),
        P(None, None, ("row", "col"), None),
        P(None, None, ("row", "col"), None),
        P(None, None, ("row", "col"), None),
        P(None, None, None, ("row", "col")),
        P(None, None, None, ("row", "col")),
        P(None, ("row", "col")),
        P(("row", "col")),
    )
    out_specs = P(None, ("row", "col"), None)
    run = functools.partial(body, mesh.shape["row"], mesh.shape["col"])
    return jax.shard_map(run, mesh=mesh, in_specs=in_specs, out_specs=out_specs, check_vma=False)
```

```python
import functools

import jax
import jax.numpy as jnp
from jax import lax
from jax.experimental import pallas as pl
from jax.experimental.pallas import tpu as pltpu
from jax.sharding import PartitionSpec as P

ITERS = 4
REACH = 2
SPAN = 2 * REACH
FAR = 2 * SPAN
PIECES = 2 * SPAN + 1
PEERS = 2 * FAR + 1
SHIFT = 1.0
CHUNK = 16
MESH = pl.DeviceIdType.MESH
F32 = jnp.float32
BF16 = jnp.bfloat16


def iota(shape, dim):
    return lax.broadcasted_iota(jnp.int32, shape, dim)


def split3(value):
    high = value.astype(BF16)
    rest = value - high.astype(F32)
    middle = rest.astype(BF16)
    low = (rest - middle.astype(F32)).astype(BF16)
    return high, middle, low


def dot(a, b):
    return lax.dot_general(a, b, (((1,), (0,)), ((), ())), preferred_element_type=F32)


def end_row(first, last):
    empty = jnp.zeros_like(first)
    return jnp.concatenate([first, empty, last, empty], axis=1)


def least_squares(hess, beta, steps):
    upper = [list(line) for line in hess]
    target = [beta] + [None] * steps
    cosines = []
    sines = []
    inverses = []
    for k in range(steps):
        for i in range(k):
            temp = cosines[i] * upper[i][k] + sines[i] * upper[i + 1][k]
            upper[i + 1][k] = cosines[i] * upper[i + 1][k] - sines[i] * upper[i][k]
            upper[i][k] = temp
        inverse = lax.rsqrt(upper[k][k] * upper[k][k] + upper[k + 1][k] * upper[k + 1][k])
        cosines.append(upper[k][k] * inverse)
        sines.append(upper[k + 1][k] * inverse)
        inverses.append(inverse)
        target[k + 1] = -sines[k] * target[k]
        target[k] = cosines[k] * target[k]
    coeffs = [None] * steps
    for k in range(steps - 1, -1, -1):
        total = target[k]
        for j in range(k + 1, steps):
            total = total - upper[k][j] * coeffs[j]
        coeffs[k] = total * inverses[k]
    return coeffs


def krylov_coeffs(gram):
    size = ITERS + 1
    low = [[None] * size for _ in range(size)]
    for j in range(size):
        total = gram[j, j]
        for k in range(j):
            total = total - low[j][k] * low[j][k]
        total = jnp.maximum(total, 1e-7 * gram[j, j])
        inverse = lax.rsqrt(total)
        low[j][j] = total * inverse
        for i in range(j + 1, size):
            total = gram[j, i]
            for k in range(j):
                total = total - low[i][k] * low[j][k]
            low[i][j] = total * inverse
    hess = [[None] * ITERS for _ in range(size)]
    for k in range(ITERS):
        for i in range(k + 2):
            hess[i][k] = low[k + 1][i]
            if i <= k:
                hess[i][k] = hess[i][k] + SHIFT * low[k][i]
    return least_squares(hess, low[0][0], ITERS)


PAIRS = [(i, j) for j in range(ITERS + 1) for i in range(j + 1)]
GRAM_ROWS = 16


def kernel(
    rows,
    columns,
    right_hbm,
    diag_hbm,
    lower_hbm,
    upper_hbm,
    precond_hbm,
    out_hbm_blocks,
    in_hbm_blocks,
    junction_hbm,
    length_hbm,
    result,
    right,
    diag,
    lower,
    upper,
    precond,
    jout,
    jin,
    junction,
    length,
    basis,
    image,
    bulk,
    sends_one,
    sends_two,
    block_sends,
    recvs_one,
    recvs_two,
    block_recvs,
    gram_own,
    gram_row,
    gram_all,
    in_sems,
    near_send,
    near_recv,
    block_send,
    block_recv,
    all_send,
    all_recv,
):
    row = lax.axis_index("row")
    col = lax.axis_index("col")

    def near(offset):
        return (row, (col + offset + columns) % columns)

    loads = [
        pltpu.make_async_copy(source, target, in_sems.at[index])
        for index, (source, target) in enumerate(
            [
                (length_hbm, length),
                (junction_hbm, junction),
                (out_hbm_blocks, jout),
                (in_hbm_blocks, jin),
                (right_hbm, right),
                (precond_hbm, precond),
                (diag_hbm, diag),
                (lower_hbm, lower),
                (upper_hbm, upper),
            ]
        )
    ]
    for load in loads:
        load.start()

    barrier = pltpu.get_barrier_semaphore()
    partners = [near(offset) for offset in range(-FAR, FAR + 1) if offset != 0]
    partners += [((row + step) % rows, col) for step in range(1, rows)]
    for partner in partners:
        pl.semaphore_signal(barrier, inc=1, device_id=partner, device_id_type=MESH)

    sends_one[...] = jnp.zeros_like(sends_one)
    sends_two[...] = jnp.zeros_like(sends_two)
    for load in loads[:6]:
        load.wait()

    lane = iota((1, 128), 1)
    lengths = length[...]
    length_row = end_row(lengths, lengths)
    slot_row = jnp.where(
        (lane & 32) != 0, -1, end_row(jnp.zeros_like(lengths), lengths - 1)
    )
    extract = (iota((256, 128), 0) == slot_row).astype(F32).astype(BF16)
    ids = junction[...]
    owned = ids % 32
    ids = (ids // 32 - col + REACH + columns) % columns * 32 + owned
    slot_of_junction_row = jnp.where((lane & 32) != 0, -1, end_row(ids[0:1], ids[1:2])).astype(F32)
    square = iota((128, 128), 0) == iota((128, 128), 1)
    slot_col = jnp.sum(jnp.where(square, slot_row.astype(F32), 0.0), axis=1, keepdims=True)
    slot_of_junction_col = jnp.sum(
        jnp.where(square, slot_of_junction_row, 0.0), axis=1, keepdims=True
    )
    insert = (iota((128, 256), 1).astype(F32) == slot_col).astype(F32)
    insert = jnp.concatenate([insert] * 3, axis=0).astype(BF16)
    length_col = jnp.sum(
        jnp.where(square[:32], length_row.astype(F32), 0.0), axis=1, keepdims=True
    )
    active = iota((32, 256), 1).astype(F32) < length_col
    single = ((length_row == 1) & ((lane & 32) == 0)).astype(F32)
    own_pipe = (iota((32, 128), 0) == (iota((32, 128), 1) & 63))[None]

    def ends_of(value):
        total = sum(dot(part, extract) for part in split3(value.reshape(128, 256)))
        return jnp.sum(jnp.where(own_pipe, total.reshape(4, 32, 128), 0.0), axis=1)

    def at_ends(value):
        spread = jnp.where(own_pipe, value[:, None, :], 0.0).reshape(128, 128)
        return dot(jnp.concatenate(split3(spread), axis=1), insert).reshape(4, 32, 256)

    def block_row(ref, a):
        return end_row(ref[0, a], ref[1, a])

    def apply(blocks, value):
        total = blocks[0] * value[0:1]
        for a in range(1, 4):
            total = total + blocks[a] * value[a : a + 1]
        return total

    out_blocks = [block_row(jout, a) for a in range(4)]
    in_blocks = [block_row(jin, a) for a in range(4)]
    pre_ends = dot(precond[...].reshape(512, 256), extract).reshape(16, 32, 128)
    pre_ends = jnp.sum(jnp.where(own_pipe, pre_ends, 0.0), axis=1)
    to_balance = [
        sum(out_blocks[a] * pre_ends[a * 4 + b : a * 4 + b + 1] for a in range(4)) for b in range(4)
    ]

    to_table = (slot_of_junction_col == iota((128, 256), 1).astype(F32)).astype(F32).astype(BF16)

    def stacked(value):
        high = value.astype(BF16).astype(F32)
        middle = (value - high).astype(BF16).astype(F32)
        low = value - high - middle
        return jnp.concatenate([high, middle, low, jnp.zeros_like(high)], axis=0).astype(BF16)

    def unstacked(total):
        return total[0:8] + total[8:16] + total[16:24]

    def eight(value):
        return jnp.concatenate([value, jnp.zeros_like(value)], axis=0)

    def post(sends, recvs, near_rows, send_sem, recv_sem, balance, free):
        table = unstacked(dot(stacked(eight(balance)), to_table))
        for version in range(4):
            shifted = pltpu.roll(table, 32 * version, 1) if version else table
            sends[version, 0:4] = shifted[0:4, :128]
            sends[version, 4:8] = shifted[0:4, 128:]
            sends[version, 8:12] = pltpu.roll(free, 32, 1) if version % 2 else free
        copies = []
        for offset in sorted(range(-FAR, FAR + 1), key=lambda o: -abs(o)):
            if offset == 0:
                continue
            count = near_rows if abs(offset) <= SPAN else 8
            copy = pltpu.make_async_remote_copy(
                src_ref=sends.at[-offset % 4, 0:count],
                dst_ref=recvs.at[FAR - offset, 0:count],
                send_sem=send_sem.at[FAR + offset],
                recv_sem=recv_sem.at[FAR + offset],
                device_id=near(offset),
                device_id_type=MESH,
            )
            copy.start()
            copies.append(copy)
        recvs[FAR, 0:near_rows] = sends[0, 0:near_rows]
        return copies

    def pieces(recvs, part):
        joined = []
        for index in range(0, PIECES, 2):
            value = recvs[SPAN + index, part]
            if index + 1 < PIECES:
                value = value + recvs[SPAN + index + 1, part]
            joined.append(value)
        return joined

    def near_balances(recvs, gather):
        starts = []
        for first in range(0, PEERS, 4):
            total = recvs[first, 0:8]
            for index in range(first + 1, min(first + 4, PEERS)):
                total = total + recvs[index, 0:8]
            starts.append(total)
        table = [starts[k + 1] + pltpu.roll(starts[k], 4, 0) for k in range(4)]
        left = stacked(jnp.concatenate(table, axis=1))
        return [
            unstacked(dot(left[:, 128 * (j // 2) : 128 * (j // 2) + 256], gather[j]))[0:4]
            for j in range(5)
        ]

    def next_balances(first, frees, blocks, crosses, matches):
        second = []
        for j in range(5):
            turned = pltpu.roll(first[j], 96, 1)
            cross = apply(crosses[j], turned)
            second.append(frees[j] + apply(blocks[j], first[j]) + pltpu.roll(cross, 96, 1))
        own = dot(stacked(eight(jnp.concatenate(second, axis=1))), matches)
        return unstacked(own)[0:4]

    def advance(step):
        if step == 0:
            for load in loads[6:]:
                load.wait()
        for first in range(0, 32, CHUNK):
            part = slice(first, first + CHUNK)
            vec = [basis[step, b, part] for b in range(4)]
            x = []
            for a in range(4):
                total = precond[a, 0, part].astype(F32) * vec[0]
                for b in range(1, 4):
                    total = total + precond[a, b, part].astype(F32) * vec[b]
                image[step, a, part] = total
                x.append(total)
            keep = active[part]
            slot = iota((CHUNK, 256), 1)
            for b in range(4):
                sums = []
                for blocks in (diag, lower, upper):
                    total = blocks[0, b, part].astype(F32) * x[0]
                    for a in range(1, 4):
                        total = total + blocks[a, b, part].astype(F32) * x[a]
                    sums.append(total)
                following = jnp.where(slot == 255, 0.0, pltpu.roll(sums[1], 255, 1))
                preceding = jnp.where(slot == 0, 0.0, pltpu.roll(sums[2], 1, 1))
                total = jnp.where(keep, sums[0] + following + preceding, 0.0)
                bulk[b, part] = total - SHIFT * vec[b]

    def inner(left, right_part):
        total = jnp.sum(left * right_part, axis=(0, 1)).reshape(1, 256)
        return total[:, :128] + total[:, 128:]

    def gram_rows(last, first_pair, last_pair):
        for index, (i, j) in enumerate(PAIRS[first_pair:last_pair], first_pair):
            gram_own[0, index : index + 1] = inner(last[i], last[j])

    half = (lane & 32) == 0
    pack = []
    for a in range(4):
        turned = pltpu.roll(in_blocks[a], 64, 1)
        own = apply(to_balance, in_blocks[a])
        cross = single * apply(to_balance, turned)
        pack.append(own + pltpu.roll(cross, 32, 1))
    pack = jnp.concatenate(pack, axis=0)
    place_row = jnp.where((lane & 32) == 0, slot_of_junction_row + 1.0, 0.0)
    for version in range(4):
        turn = 32 * (version % 2)
        sends_one[version, 12:13] = pltpu.roll(place_row, turn, 1) if turn else place_row
    block_sends[0] = pack
    block_sends[1] = pltpu.roll(pack, 32, 1)

    start = jnp.where(active[None], right[...], 0.0)
    basis[0] = start
    balance = apply(to_balance, ends_of(start))
    advance(0)
    free = apply(to_balance, ends_of(bulk[...]))
    pl.semaphore_wait(barrier, len(partners))
    copies = post(sends_one, recvs_one, 13, near_send.at[0], near_recv.at[0], balance, free)
    block_copies = []
    for offset in sorted(range(-SPAN, SPAN + 1), key=lambda o: -abs(o)):
        if offset != 0:
            copy = pltpu.make_async_remote_copy(
                src_ref=block_sends.at[offset % 2],
                dst_ref=block_recvs.at[SPAN - offset],
                send_sem=block_send.at[SPAN + offset],
                recv_sem=block_recv.at[SPAN + offset],
                device_id=near(offset),
                device_id_type=MESH,
            )
            copy.start()
            block_copies.append(copy)
    block_recvs[SPAN] = block_sends[0]
    pending = copies + block_copies
    for copy in copies:
        copy.wait_recv()

    joined = pieces(recvs_one, slice(8, 13))
    gather = []
    place_rows = []
    for j in range(5):
        tagged = joined[j][4:5]
        column = 2.0 * j + jnp.where(half, 0.0, 1.0)
        position = jnp.where(tagged > 0.5, tagged - 1.0 + 32.0 * column, -1000.0)
        place_rows.append(position)
        rows_of = iota((256, 128), 0).astype(F32) + 128.0 * (j // 2)
        gather.append((rows_of == position).astype(F32).astype(BF16))
    own_place = jnp.where(slot_of_junction_col < 0.0, -2000.0, slot_of_junction_col + 128.0)
    matches = (own_place == jnp.concatenate(place_rows, axis=1)).astype(F32).T.astype(BF16)
    first = near_balances(recvs_one, gather)
    for copy in block_copies:
        copy.wait_recv()
    blocks = []
    crosses = []
    for index in range(0, PIECES, 2):
        even = block_recvs[index]
        odd = block_recvs[index + 1] if index + 1 < PIECES else jnp.zeros_like(even)
        own = jnp.where(half, even, odd)
        cross = jnp.where(half, odd, even)
        blocks.append([own[4 * a : 4 * a + 4] for a in range(4)])
        crosses.append([cross[4 * a : 4 * a + 4] for a in range(4)])

    second = next_balances(first, [value[0:4] for value in joined], blocks, crosses, matches)
    basis[1] = bulk[...] + at_ends(apply(in_blocks, first[2]))
    advance(1)
    basis[2] = bulk[...] + at_ends(apply(in_blocks, second))
    balance = apply(to_balance, ends_of(basis[2]))
    advance(2)
    free = apply(to_balance, ends_of(bulk[...]))
    copies = post(sends_two, recvs_two, 12, near_send.at[1], near_recv.at[1], balance, free)
    pending += copies
    gram_rows(basis, 0, 6)
    gram_own[0, len(PAIRS) : GRAM_ROWS] = jnp.zeros((GRAM_ROWS - len(PAIRS), 128), F32)
    for copy in copies:
        copy.wait_recv()

    joined = pieces(recvs_two, slice(8, 12))
    first = near_balances(recvs_two, gather)
    second = next_balances(first, joined, blocks, crosses, matches)
    basis[3] = bulk[...] + at_ends(apply(in_blocks, first[2]))
    advance(3)
    basis[4] = bulk[...] + at_ends(apply(in_blocks, second))
    gram_rows(basis, 6, len(PAIRS))

    partial = jnp.sum(gram_own[0], axis=1, keepdims=True)
    eye = iota((GRAM_ROWS, 128), 0) == iota((GRAM_ROWS, 128), 1)
    mine = row * columns + col
    gram_row[0] = jnp.sum(jnp.where(eye, partial, 0.0), axis=0, keepdims=True)
    gram_all[mine] = gram_row[0]
    others = rows * columns - 1

    def tell(index, carry):
        target = index + jnp.where(index >= mine, 1, 0)
        pltpu.make_async_remote_copy(
            src_ref=gram_row.at[0],
            dst_ref=gram_all.at[mine],
            send_sem=all_send,
            recv_sem=all_recv,
            device_id=(target // columns, target % columns),
            device_id_type=MESH,
        ).start()
        return carry

    lax.fori_loop(0, others, tell, 0, unroll=5)
    received = gram_all.at[0:others]
    pltpu.make_async_copy(received, received, all_recv).wait()
    total = jnp.sum(gram_all[...], axis=0)
    splat = jnp.sum(jnp.where(eye, total, 0.0), axis=1, keepdims=True)
    splat = jnp.broadcast_to(splat, (GRAM_ROWS, 128))
    gram = {
        pair: jnp.broadcast_to(splat[index : index + 1], (8, 128))
        for index, pair in enumerate(PAIRS)
    }
    coeffs = [jnp.broadcast_to(value[0:1], (32, 128)) for value in krylov_coeffs(gram)]
    for a in range(4):
        for lanes in (slice(0, 128), slice(128, 256)):
            value = coeffs[0] * image[0, a, :, lanes]
            for k in range(1, ITERS):
                value = value + coeffs[k] * image[k, a, :, lanes]
            result[a, :, lanes] = value
    for copy in pending:
        copy.wait_send()
    pltpu.make_async_copy(received, received, all_send).wait()


def body(rows, columns, right_side, diag, lower, upper, precond, jout, jin, junction, length):
    pipes, slots = right_side.shape[1:]
    length = length.reshape(1, pipes)
    operands = (right_side, diag, lower, upper, precond, jout, jin, junction, length)
    held = [pltpu.with_memory_space_constraint(value, pltpu.HBM) for value in operands]
    inputs = [pltpu.VMEM(value.shape, value.dtype) for value in operands]
    return pl.pallas_call(
        functools.partial(kernel, rows, columns),
        out_shape=pltpu.VMEM(right_side.shape, F32),
        in_specs=[pl.BlockSpec(memory_space=pltpu.HBM)] * len(operands),
        out_specs=pl.BlockSpec(memory_space=pltpu.VMEM),
        scratch_shapes=inputs
        + [
            pltpu.VMEM((ITERS + 1, 4, pipes, slots), F32),
            pltpu.VMEM((ITERS, 4, pipes, slots), F32),
            pltpu.VMEM((4, pipes, slots), F32),
            pltpu.VMEM((4, 16, 128), F32),
            pltpu.VMEM((4, 16, 128), F32),
            pltpu.VMEM((2, 16, 128), F32),
            pltpu.VMEM((PEERS, 16, 128), F32),
            pltpu.VMEM((PEERS, 16, 128), F32),
            pltpu.VMEM((PIECES, 16, 128), F32),
            pltpu.VMEM((1, GRAM_ROWS, 128), F32),
            pltpu.VMEM((1, 1, 128), F32),
            pltpu.VMEM((rows * columns, 1, 128), F32),
            pltpu.SemaphoreType.DMA((len(operands),)),
            pltpu.SemaphoreType.DMA((2, PEERS)),
            pltpu.SemaphoreType.DMA((2, PEERS)),
            pltpu.SemaphoreType.DMA((PIECES,)),
            pltpu.SemaphoreType.DMA((PIECES,)),
            pltpu.SemaphoreType.DMA,
            pltpu.SemaphoreType.DMA,
        ],
        compiler_params=pltpu.CompilerParams(
            collective_id=0, has_side_effects=True, vmem_limit_bytes=48 * 1024 * 1024
        ),
    )(*held)


def solution(mesh):
    in_specs = (
        P(None, ("row", "col"), None),
        P(None, None, ("row", "col"), None),
        P(None, None, ("row", "col"), None),
        P(None, None, ("row", "col"), None),
        P(None, None, ("row", "col"), None),
        P(None, None, None, ("row", "col")),
        P(None, None, None, ("row", "col")),
        P(None, ("row", "col")),
        P(("row", "col")),
    )
    out_specs = P(None, ("row", "col"), None)
    run = functools.partial(body, mesh.shape["row"], mesh.shape["col"])
    return jax.shard_map(run, mesh=mesh, in_specs=in_specs, out_specs=out_specs, check_vma=False)
```

```python
import functools

import jax
import jax.numpy as jnp
from jax import lax
from jax.experimental import pallas as pl
from jax.experimental.pallas import tpu as pltpu
from jax.sharding import PartitionSpec as P

ITERS = 4
REACH = 2
SPAN = 2 * REACH
FAR = 2 * SPAN
PIECES = 2 * SPAN + 1
PEERS = 2 * FAR + 1
SHIFT = 1.0
CHUNK = 16
MESH = pl.DeviceIdType.MESH
F32 = jnp.float32
BF16 = jnp.bfloat16


def iota(shape, dim):
    return lax.broadcasted_iota(jnp.int32, shape, dim)


def split3(value):
    high = value.astype(BF16)
    rest = value - high.astype(F32)
    middle = rest.astype(BF16)
    low = (rest - middle.astype(F32)).astype(BF16)
    return high, middle, low


def dot(a, b):
    return lax.dot_general(a, b, (((1,), (0,)), ((), ())), preferred_element_type=F32)


def end_row(first, last):
    empty = jnp.zeros_like(first)
    return jnp.concatenate([first, empty, last, empty], axis=1)


def least_squares(hess, beta, steps):
    upper = [list(line) for line in hess]
    target = [beta] + [None] * steps
    cosines = []
    sines = []
    inverses = []
    for k in range(steps):
        for i in range(k):
            temp = cosines[i] * upper[i][k] + sines[i] * upper[i + 1][k]
            upper[i + 1][k] = cosines[i] * upper[i + 1][k] - sines[i] * upper[i][k]
            upper[i][k] = temp
        inverse = lax.rsqrt(upper[k][k] * upper[k][k] + upper[k + 1][k] * upper[k + 1][k])
        cosines.append(upper[k][k] * inverse)
        sines.append(upper[k + 1][k] * inverse)
        inverses.append(inverse)
        target[k + 1] = -sines[k] * target[k]
        target[k] = cosines[k] * target[k]
    coeffs = [None] * steps
    for k in range(steps - 1, -1, -1):
        total = target[k]
        for j in range(k + 1, steps):
            total = total - upper[k][j] * coeffs[j]
        coeffs[k] = total * inverses[k]
    return coeffs


def krylov_coeffs(gram):
    size = ITERS + 1
    low = [[None] * size for _ in range(size)]
    for j in range(size):
        total = gram[j, j]
        for k in range(j):
            total = total - low[j][k] * low[j][k]
        total = jnp.maximum(total, 1e-7 * gram[j, j])
        inverse = lax.rsqrt(total)
        low[j][j] = total * inverse
        for i in range(j + 1, size):
            total = gram[j, i]
            for k in range(j):
                total = total - low[i][k] * low[j][k]
            low[i][j] = total * inverse
    hess = [[None] * ITERS for _ in range(size)]
    for k in range(ITERS):
        for i in range(k + 2):
            hess[i][k] = low[k + 1][i]
            if i <= k:
                hess[i][k] = hess[i][k] + SHIFT * low[k][i]
    return least_squares(hess, low[0][0], ITERS)


PAIRS = [(i, j) for j in range(ITERS + 1) for i in range(j + 1)]
GRAM_ROWS = 16


def kernel(
    rows,
    columns,
    right_hbm,
    diag_hbm,
    lower_hbm,
    upper_hbm,
    precond_hbm,
    out_hbm_blocks,
    in_hbm_blocks,
    junction_hbm,
    length_hbm,
    result,
    right,
    diag,
    lower,
    upper,
    precond,
    jout,
    jin,
    junction,
    length,
    basis,
    image,
    bulk,
    spare,
    sends_one,
    sends_two,
    block_sends,
    recvs_one,
    recvs_two,
    block_recvs,
    gram_own,
    gram_row,
    gram_all,
    in_sems,
    near_send,
    near_recv,
    block_send,
    block_recv,
    all_send,
    all_recv,
):
    row = lax.axis_index("row")
    col = lax.axis_index("col")

    def near(offset):
        return (row, (col + offset + columns) % columns)

    barrier = pltpu.get_barrier_semaphore()
    partners = [near(offset) for offset in range(-FAR, FAR + 1) if offset != 0]
    partners += [((row + step) % rows, col) for step in range(1, rows)]
    for partner in partners:
        pl.semaphore_signal(barrier, inc=1, device_id=partner, device_id_type=MESH)

    loads = [
        pltpu.make_async_copy(source, target, in_sems.at[index])
        for index, (source, target) in enumerate(
            [
                (length_hbm, length),
                (junction_hbm, junction),
                (out_hbm_blocks, jout),
                (in_hbm_blocks, jin),
                (right_hbm, right),
                (precond_hbm, precond),
                (diag_hbm, diag),
                (lower_hbm, lower),
                (upper_hbm, upper),
            ]
        )
    ]
    for load in loads:
        load.start()

    sends_one[...] = jnp.zeros_like(sends_one)
    sends_two[...] = jnp.zeros_like(sends_two)
    for load in loads[:2]:
        load.wait()

    lane = iota((1, 128), 1)
    lengths = length[...]
    length_row = end_row(lengths, lengths)
    slot_row = jnp.where(
        (lane & 32) != 0, -1, end_row(jnp.zeros_like(lengths), lengths - 1)
    )
    extract = (iota((256, 128), 0) == slot_row).astype(F32).astype(BF16)
    ids = junction[...]
    owned = ids % 32
    ids = (ids // 32 - col + REACH + columns) % columns * 32 + owned
    slot_of_junction_row = jnp.where((lane & 32) != 0, -1, end_row(ids[0:1], ids[1:2])).astype(F32)
    square = iota((128, 128), 0) == iota((128, 128), 1)
    slot_col = jnp.sum(jnp.where(square, slot_row.astype(F32), 0.0), axis=1, keepdims=True)
    slot_of_junction_col = jnp.sum(
        jnp.where(square, slot_of_junction_row, 0.0), axis=1, keepdims=True
    )
    insert = (iota((128, 256), 1).astype(F32) == slot_col).astype(F32)
    insert = jnp.concatenate([insert] * 3, axis=0).astype(BF16)
    length_col = jnp.sum(
        jnp.where(square[:32], length_row.astype(F32), 0.0), axis=1, keepdims=True
    )
    active = iota((32, 256), 1).astype(F32) < length_col
    single = ((length_row == 1) & ((lane & 32) == 0)).astype(F32)
    own_pipe = (iota((32, 128), 0) == (iota((32, 128), 1) & 63))[None]

    def ends_of(value):
        total = sum(dot(part, extract) for part in split3(value.reshape(128, 256)))
        return jnp.sum(jnp.where(own_pipe, total.reshape(4, 32, 128), 0.0), axis=1)

    def at_ends(value):
        spread = jnp.where(own_pipe, value[:, None, :], 0.0).reshape(128, 128)
        return dot(jnp.concatenate(split3(spread), axis=1), insert).reshape(4, 32, 256)

    def block_row(ref, a):
        return end_row(ref[0, a], ref[1, a])

    def apply(blocks, value):
        total = blocks[0] * value[0:1]
        for a in range(1, 4):
            total = total + blocks[a] * value[a : a + 1]
        return total

    for load in loads[2:6]:
        load.wait()
    out_blocks = [block_row(jout, a) for a in range(4)]
    in_blocks = [block_row(jin, a) for a in range(4)]

    def block_ends(blocks, at):
        total = dot(blocks, at).reshape(16, 32, 128)
        total = jnp.sum(jnp.where(own_pipe, total, 0.0), axis=1)
        return [total[4 * a : 4 * a + 4] for a in range(4)]

    pre_blocks = jnp.concatenate([precond[a, b] for b in range(4) for a in range(4)], axis=0)
    pre_ends = block_ends(pre_blocks, extract)
    to_balance = [
        sum(out_blocks[a] * pre_ends[b][a : a + 1] for a in range(4)) for b in range(4)
    ]

    to_table = (slot_of_junction_col == iota((128, 256), 1).astype(F32)).astype(F32).astype(BF16)

    def stacked(value):
        high = value.astype(BF16).astype(F32)
        middle = (value - high).astype(BF16).astype(F32)
        low = value - high - middle
        return jnp.concatenate([high, middle, low, jnp.zeros_like(high)], axis=0).astype(BF16)

    def unstacked(total):
        return total[0:8] + total[8:16] + total[16:24]

    def eight(value):
        return jnp.concatenate([value, jnp.zeros_like(value)], axis=0)

    def fill(sends, balance, free):
        table = unstacked(dot(stacked(eight(balance)), to_table))
        for version in range(4):
            shifted = pltpu.roll(table, 32 * version, 1) if version else table
            sends[version, 0:4] = shifted[0:4, :128]
            sends[version, 4:8] = shifted[0:4, 128:]
            sends[version, 8:12] = pltpu.roll(free, 32, 1) if version % 2 else free

    def post(sends, recvs, near_rows, send_sem, recv_sem):
        copies = []
        for offset in sorted(range(-FAR, FAR + 1), key=lambda o: -abs(o)):
            if offset == 0:
                continue
            count = near_rows if abs(offset) <= SPAN else 8
            copy = pltpu.make_async_remote_copy(
                src_ref=sends.at[-offset % 4, 0:count],
                dst_ref=recvs.at[FAR - offset, 0:count],
                send_sem=send_sem.at[FAR + offset],
                recv_sem=recv_sem.at[FAR + offset],
                device_id=near(offset),
                device_id_type=MESH,
            )
            copy.start()
            copies.append(copy)
        recvs[FAR, 0:near_rows] = sends[0, 0:near_rows]
        return copies

    def pieces(recvs, part):
        joined = []
        for index in range(0, PIECES, 2):
            value = recvs[SPAN + index, part]
            if index + 1 < PIECES:
                value = value + recvs[SPAN + index + 1, part]
            joined.append(value)
        return joined

    def near_balances(recvs, gather):
        starts = []
        for first in range(0, PEERS, 4):
            total = recvs[first, 0:8]
            for index in range(first + 1, min(first + 4, PEERS)):
                total = total + recvs[index, 0:8]
            starts.append(total)
        table = [starts[k + 1] + pltpu.roll(starts[k], 4, 0) for k in range(4)]
        left = stacked(jnp.concatenate(table, axis=1))
        return [
            unstacked(dot(left[:, 128 * (j // 2) : 128 * (j // 2) + 256], gather[j]))[0:4]
            for j in range(5)
        ]

    def next_balances(first, frees, blocks, crosses, matches):
        second = []
        for j in range(5):
            turned = pltpu.roll(first[j], 96, 1)
            cross = apply(crosses[j], turned)
            second.append(frees[j] + apply(blocks[j], first[j]) + pltpu.roll(cross, 96, 1))
        own = dot(stacked(eight(jnp.concatenate(second, axis=1))), matches)
        return unstacked(own)[0:4]

    def advance(source, target, picture=None):
        for first in range(0, 32, CHUNK):
            part = slice(first, first + CHUNK)
            vec = [source[b, part] for b in range(4)]
            x = []
            for a in range(4):
                total = precond[a, 0, part].astype(F32) * vec[0]
                for b in range(1, 4):
                    total = total + precond[a, b, part].astype(F32) * vec[b]
                if picture is not None:
                    picture[a, part] = total
                x.append(total)
            keep = active[part]
            slot = iota((CHUNK, 256), 1)
            for b in range(4):
                sums = []
                for blocks in (diag, lower, upper):
                    total = blocks[0, b, part].astype(F32) * x[0]
                    for a in range(1, 4):
                        total = total + blocks[a, b, part].astype(F32) * x[a]
                    sums.append(total)
                following = jnp.where(slot == 255, 0.0, pltpu.roll(sums[1], 255, 1))
                preceding = jnp.where(slot == 0, 0.0, pltpu.roll(sums[2], 1, 1))
                total = jnp.where(keep, sums[0] + following + preceding, 0.0)
                target[b, part] = total - SHIFT * vec[b]

    def inner(left, right_part):
        total = jnp.sum(left * right_part, axis=(0, 1)).reshape(1, 256)
        return total[:, :128] + total[:, 128:]

    def gram_rows(last, first_pair, last_pair):
        for index, (i, j) in enumerate(PAIRS[first_pair:last_pair], first_pair):
            gram_own[0, index : index + 1] = inner(last[i], last[j])

    half = (lane & 32) == 0
    pack = []
    for a in range(4):
        turned = pltpu.roll(in_blocks[a], 64, 1)
        own = apply(to_balance, in_blocks[a])
        cross = single * apply(to_balance, turned)
        pack.append(own + pltpu.roll(cross, 32, 1))
    pack = jnp.concatenate(pack, axis=0)
    place_row = jnp.where((lane & 32) == 0, slot_of_junction_row + 1.0, 0.0)
    for version in range(4):
        turn = 32 * (version % 2)
        sends_one[version, 12:13] = pltpu.roll(place_row, turn, 1) if turn else place_row
    block_sends[0] = pack
    block_sends[1] = pltpu.roll(pack, 32, 1)

    start = jnp.where(active[None], right[...], 0.0)
    basis[0] = start
    balance = apply(to_balance, ends_of(start))
    for load in loads[6:]:
        load.wait()
    advance(basis.at[0], bulk, image.at[0])
    bulk_ends = ends_of(bulk[...])
    free = apply(to_balance, bulk_ends)
    fill(sends_one, balance, free)
    pl.semaphore_wait(barrier, len(partners))
    copies = post(sends_one, recvs_one, 13, near_send.at[0], near_recv.at[0])
    block_copies = []
    for offset in sorted(range(-SPAN, SPAN + 1), key=lambda o: -abs(o)):
        if offset != 0:
            copy = pltpu.make_async_remote_copy(
                src_ref=block_sends.at[offset % 2],
                dst_ref=block_recvs.at[SPAN - offset],
                send_sem=block_send.at[SPAN + offset],
                recv_sem=block_recv.at[SPAN + offset],
                device_id=near(offset),
                device_id_type=MESH,
            )
            copy.start()
            block_copies.append(copy)
    block_recvs[SPAN] = block_sends[0]
    pending = copies + block_copies

    advance(bulk, spare.at[0])
    spare_ends = ends_of(spare[0])
    advance(spare.at[0], spare.at[1])
    far_ends = ends_of(spare[1])
    is_first = lane < 64
    used = (lane & 32) == 0
    extracts = [extract]
    for depth in (1, 2):
        slot = jnp.where(is_first, depth, length_row - 1 - depth)
        slot = jnp.where(used & (length_row > depth), slot, -1)
        extracts.append((iota((256, 128), 0) == slot).astype(F32).astype(BF16))
    pre_at = [pre_ends] + [block_ends(pre_blocks, extracts[d]) for d in (1, 2)]
    diag_at = [block_ends(diag[...].reshape(512, 256), extracts[d]) for d in (0, 1)]
    lower_at = [block_ends(lower[...].reshape(512, 256), extracts[d]) for d in range(3)]
    upper_at = [block_ends(upper[...].reshape(512, 256), extracts[d]) for d in range(3)]
    inward = [None] + [
        [jnp.where(is_first, lower_at[d][a], upper_at[d][a]) for a in range(4)] for d in (1, 2)
    ]
    outward = [
        [
            jnp.where(
                length_row > d + 1, jnp.where(is_first, upper_at[d][a], lower_at[d][a]), 0.0
            )
            for a in range(4)
        ]
        for d in (0, 1)
    ]
    of_length = [((length_row == count) & used).astype(F32) for count in (1, 2, 3)]

    def at_depths(added):
        other = pltpu.roll(added, 64, 1)
        return [added + of_length[0] * other, of_length[1] * other, of_length[2] * other]

    def step_at_end(value):
        x = [apply(pre_at[d], value[d]) for d in (0, 1)]
        return apply(diag_at[0], x[0]) + apply(inward[1], x[1]) - SHIFT * value[0]

    def step_at_ends(value):
        x = [apply(pre_at[d], value[d]) for d in range(3)]
        return [
            apply(diag_at[0], x[0]) + apply(inward[1], x[1]) - SHIFT * value[0],
            apply(diag_at[1], x[1])
            + apply(outward[0], x[0])
            + apply(inward[2], x[2])
            - SHIFT * value[1],
        ]

    for copy in copies:
        copy.wait_recv()

    joined = pieces(recvs_one, slice(8, 13))
    gather = []
    place_rows = []
    for j in range(5):
        tagged = joined[j][4:5]
        column = 2.0 * j + jnp.where(half, 0.0, 1.0)
        position = jnp.where(tagged > 0.5, tagged - 1.0 + 32.0 * column, -1000.0)
        place_rows.append(position)
        rows_of = iota((256, 128), 0).astype(F32) + 128.0 * (j // 2)
        gather.append((rows_of == position).astype(F32).astype(BF16))
    own_place = jnp.where(slot_of_junction_col < 0.0, -2000.0, slot_of_junction_col + 128.0)
    matches = (own_place == jnp.concatenate(place_rows, axis=1)).astype(F32).T.astype(BF16)
    first = near_balances(recvs_one, gather)
    for copy in block_copies:
        copy.wait_recv()
    blocks = []
    crosses = []
    for index in range(0, PIECES, 2):
        even = block_recvs[index]
        odd = block_recvs[index + 1] if index + 1 < PIECES else jnp.zeros_like(even)
        own = jnp.where(half, even, odd)
        cross = jnp.where(half, odd, even)
        blocks.append([own[4 * a : 4 * a + 4] for a in range(4)])
        crosses.append([cross[4 * a : 4 * a + 4] for a in range(4)])

    second = next_balances(first, [value[0:4] for value in joined], blocks, crosses, matches)
    added_one = apply(in_blocks, first[2])
    added_two = apply(in_blocks, second)
    moved = step_at_ends(at_depths(added_one))
    moved = [value + more for value, more in zip(moved, at_depths(added_two))]
    balance = apply(to_balance, spare_ends + moved[0])
    free = apply(to_balance, far_ends + step_at_end(moved))
    fill(sends_two, balance, free)
    copies = post(sends_two, recvs_two, 12, near_send.at[1], near_recv.at[1])
    pending += copies
    basis[1] = bulk[...] + at_ends(added_one)
    advance(basis.at[1], bulk, image.at[1])
    basis[2] = bulk[...] + at_ends(added_two)
    advance(basis.at[2], bulk, image.at[2])
    gram_rows(basis, 0, 6)
    gram_own[0, len(PAIRS) : GRAM_ROWS] = jnp.zeros((GRAM_ROWS - len(PAIRS), 128), F32)
    for copy in copies:
        copy.wait_recv()

    joined = pieces(recvs_two, slice(8, 12))
    first = near_balances(recvs_two, gather)
    second = next_balances(first, joined, blocks, crosses, matches)
    basis[3] = bulk[...] + at_ends(apply(in_blocks, first[2]))
    advance(basis.at[3], bulk, image.at[3])
    basis[4] = bulk[...] + at_ends(apply(in_blocks, second))
    gram_rows(basis, 6, len(PAIRS))

    partial = jnp.sum(gram_own[0], axis=1, keepdims=True)
    eye = iota((GRAM_ROWS, 128), 0) == iota((GRAM_ROWS, 128), 1)
    mine = row * columns + col
    gram_row[0] = jnp.sum(jnp.where(eye, partial, 0.0), axis=0, keepdims=True)
    gram_all[mine] = gram_row[0]
    others = rows * columns - 1

    def tell(index, carry):
        target = index + jnp.where(index >= row * columns, 1, 0)
        pltpu.make_async_remote_copy(
            src_ref=gram_row.at[0],
            dst_ref=gram_all.at[mine],
            send_sem=all_send,
            recv_sem=all_recv,
            device_id=(target // columns, (col + target) % columns),
            device_id_type=MESH,
        ).start()
        return carry

    lax.fori_loop(0, others, tell, 0, unroll=5)
    received = gram_all.at[0:others]
    pltpu.make_async_copy(received, received, all_recv).wait()
    total = jnp.sum(gram_all[...], axis=0)
    splat = jnp.sum(jnp.where(eye, total, 0.0), axis=1, keepdims=True)
    splat = jnp.broadcast_to(splat, (GRAM_ROWS, 128))
    gram = {
        pair: jnp.broadcast_to(splat[index : index + 1], (8, 128))
        for index, pair in enumerate(PAIRS)
    }
    coeffs = [jnp.broadcast_to(value[0:1], (32, 128)) for value in krylov_coeffs(gram)]
    for a in range(4):
        for lanes in (slice(0, 128), slice(128, 256)):
            value = coeffs[0] * image[0, a, :, lanes]
            for k in range(1, ITERS):
                value = value + coeffs[k] * image[k, a, :, lanes]
            result[a, :, lanes] = value
    for copy in pending:
        copy.wait_send()
    pltpu.make_async_copy(received, received, all_send).wait()


def body(rows, columns, right_side, diag, lower, upper, precond, jout, jin, junction, length):
    pipes, slots = right_side.shape[1:]
    length = length.reshape(1, pipes)
    operands = (right_side, diag, lower, upper, precond, jout, jin, junction, length)
    held = [pltpu.with_memory_space_constraint(value, pltpu.HBM) for value in operands]
    inputs = [pltpu.VMEM(value.shape, value.dtype) for value in operands]
    return pl.pallas_call(
        functools.partial(kernel, rows, columns),
        out_shape=pltpu.VMEM(right_side.shape, F32),
        in_specs=[pl.BlockSpec(memory_space=pltpu.HBM)] * len(operands),
        out_specs=pl.BlockSpec(memory_space=pltpu.VMEM),
        scratch_shapes=inputs
        + [
            pltpu.VMEM((ITERS + 1, 4, pipes, slots), F32),
            pltpu.VMEM((ITERS, 4, pipes, slots), F32),
            pltpu.VMEM((4, pipes, slots), F32),
            pltpu.VMEM((2, 4, pipes, slots), F32),
            pltpu.VMEM((4, 16, 128), F32),
            pltpu.VMEM((4, 16, 128), F32),
            pltpu.VMEM((2, 16, 128), F32),
            pltpu.VMEM((PEERS, 16, 128), F32),
            pltpu.VMEM((PEERS, 16, 128), F32),
            pltpu.VMEM((PIECES, 16, 128), F32),
            pltpu.VMEM((1, GRAM_ROWS, 128), F32),
            pltpu.VMEM((1, 1, 128), F32),
            pltpu.VMEM((rows * columns, 1, 128), F32),
            pltpu.SemaphoreType.DMA((len(operands),)),
            pltpu.SemaphoreType.DMA((2, PEERS)),
            pltpu.SemaphoreType.DMA((2, PEERS)),
            pltpu.SemaphoreType.DMA((PIECES,)),
            pltpu.SemaphoreType.DMA((PIECES,)),
            pltpu.SemaphoreType.DMA,
            pltpu.SemaphoreType.DMA,
        ],
        compiler_params=pltpu.CompilerParams(
            collective_id=0, has_side_effects=True, vmem_limit_bytes=48 * 1024 * 1024
        ),
    )(*held)


def solution(mesh):
    in_specs = (
        P(None, ("row", "col"), None),
        P(None, None, ("row", "col"), None),
        P(None, None, ("row", "col"), None),
        P(None, None, ("row", "col"), None),
        P(None, None, ("row", "col"), None),
        P(None, None, None, ("row", "col")),
        P(None, None, None, ("row", "col")),
        P(None, ("row", "col")),
        P(("row", "col")),
    )
    out_specs = P(None, ("row", "col"), None)
    run = functools.partial(body, mesh.shape["row"], mesh.shape["col"])
    return jax.shard_map(run, mesh=mesh, in_specs=in_specs, out_specs=out_specs, check_vma=False)
```

```python
import functools

import jax
import jax.numpy as jnp
from jax import lax
from jax.experimental import pallas as pl
from jax.experimental.pallas import tpu as pltpu
from jax.sharding import PartitionSpec as P

ITERS = 4
REACH = 2
SPAN = 2 * REACH
FAR = 2 * SPAN
PIECES = 2 * SPAN + 1
PEERS = 2 * FAR + 1
SHIFT = 1.0
CHUNK = 16
MESH = pl.DeviceIdType.MESH
F32 = jnp.float32
BF16 = jnp.bfloat16


def iota(shape, dim):
    return lax.broadcasted_iota(jnp.int32, shape, dim)


def split3(value):
    high = value.astype(BF16)
    rest = value - high.astype(F32)
    middle = rest.astype(BF16)
    low = (rest - middle.astype(F32)).astype(BF16)
    return high, middle, low


def dot(a, b):
    return lax.dot_general(a, b, (((1,), (0,)), ((), ())), preferred_element_type=F32)


def end_row(first, last):
    empty = jnp.zeros_like(first)
    return jnp.concatenate([first, empty, last, empty], axis=1)


def least_squares(hess, beta, steps):
    upper = [list(line) for line in hess]
    target = [beta] + [None] * steps
    cosines = []
    sines = []
    inverses = []
    for k in range(steps):
        for i in range(k):
            temp = cosines[i] * upper[i][k] + sines[i] * upper[i + 1][k]
            upper[i + 1][k] = cosines[i] * upper[i + 1][k] - sines[i] * upper[i][k]
            upper[i][k] = temp
        inverse = lax.rsqrt(upper[k][k] * upper[k][k] + upper[k + 1][k] * upper[k + 1][k])
        cosines.append(upper[k][k] * inverse)
        sines.append(upper[k + 1][k] * inverse)
        inverses.append(inverse)
        target[k + 1] = -sines[k] * target[k]
        target[k] = cosines[k] * target[k]
    coeffs = [None] * steps
    for k in range(steps - 1, -1, -1):
        total = target[k]
        for j in range(k + 1, steps):
            total = total - upper[k][j] * coeffs[j]
        coeffs[k] = total * inverses[k]
    return coeffs


def krylov_coeffs(gram):
    size = ITERS + 1
    low = [[None] * size for _ in range(size)]
    for j in range(size):
        total = gram[j, j]
        for k in range(j):
            total = total - low[j][k] * low[j][k]
        total = jnp.maximum(total, 1e-7 * gram[j, j])
        inverse = lax.rsqrt(total)
        low[j][j] = total * inverse
        for i in range(j + 1, size):
            total = gram[j, i]
            for k in range(j):
                total = total - low[i][k] * low[j][k]
            low[i][j] = total * inverse
    hess = [[None] * ITERS for _ in range(size)]
    for k in range(ITERS):
        for i in range(k + 2):
            hess[i][k] = low[k + 1][i]
            if i <= k:
                hess[i][k] = hess[i][k] + SHIFT * low[k][i]
    return least_squares(hess, low[0][0], ITERS)


PAIRS = [(i, j) for j in range(ITERS + 1) for i in range(j + 1)]
GRAM_ROWS = 16


def kernel(
    rows,
    columns,
    right_hbm,
    diag_hbm,
    lower_hbm,
    upper_hbm,
    precond_hbm,
    out_hbm_blocks,
    in_hbm_blocks,
    junction_hbm,
    length_hbm,
    result,
    right,
    diag,
    lower,
    upper,
    precond,
    jout,
    jin,
    junction,
    length,
    basis,
    image,
    bulk,
    spare,
    sends_one,
    sends_two,
    block_sends,
    recvs_one,
    recvs_two,
    block_recvs,
    gram_own,
    gram_row,
    gram_all,
    in_sems,
    near_send,
    near_recv,
    block_send,
    block_recv,
    all_send,
    all_recv,
):
    row = lax.axis_index("row")
    col = lax.axis_index("col")

    def near(offset):
        return (row, (col + offset + columns) % columns)

    barrier = pltpu.get_barrier_semaphore()
    partners = [near(offset) for offset in range(-FAR, FAR + 1) if offset != 0]
    partners += [((row + step) % rows, col) for step in range(1, rows)]
    for partner in partners:
        pl.semaphore_signal(barrier, inc=1, device_id=partner, device_id_type=MESH)

    loads = [
        pltpu.make_async_copy(source, target, in_sems.at[index])
        for index, (source, target) in enumerate(
            [
                (length_hbm, length),
                (junction_hbm, junction),
                (out_hbm_blocks, jout),
                (in_hbm_blocks, jin),
                (right_hbm, right),
                (precond_hbm, precond),
                (diag_hbm, diag),
                (lower_hbm, lower),
                (upper_hbm, upper),
            ]
        )
    ]
    for load in loads:
        load.start()

    sends_one[...] = jnp.zeros_like(sends_one)
    sends_two[...] = jnp.zeros_like(sends_two)
    for load in loads[:2]:
        load.wait()

    lane = iota((1, 128), 1)
    lengths = length[...]
    length_row = end_row(lengths, lengths)
    slot_row = jnp.where(
        (lane & 32) != 0, -1, end_row(jnp.zeros_like(lengths), lengths - 1)
    )
    extract = (iota((256, 128), 0) == slot_row).astype(F32).astype(BF16)
    ids = junction[...]
    owned = ids % 32
    ids = (ids // 32 - col + REACH + columns) % columns * 32 + owned
    slot_of_junction_row = jnp.where((lane & 32) != 0, -1, end_row(ids[0:1], ids[1:2])).astype(F32)
    square = iota((128, 128), 0) == iota((128, 128), 1)
    slot_col = jnp.sum(jnp.where(square, slot_row.astype(F32), 0.0), axis=1, keepdims=True)
    slot_of_junction_col = jnp.sum(
        jnp.where(square, slot_of_junction_row, 0.0), axis=1, keepdims=True
    )
    insert = (iota((128, 256), 1).astype(F32) == slot_col).astype(F32)
    insert = jnp.concatenate([insert] * 3, axis=0).astype(BF16)
    length_col = jnp.sum(
        jnp.where(square[:32], length_row.astype(F32), 0.0), axis=1, keepdims=True
    )
    active = iota((32, 256), 1).astype(F32) < length_col
    single = ((length_row == 1) & ((lane & 32) == 0)).astype(F32)
    own_pipe = (iota((32, 128), 0) == (iota((32, 128), 1) & 63))[None]

    def ends_of(value, at=extract):
        total = sum(dot(part, at) for part in split3(value.reshape(128, 256)))
        return jnp.sum(jnp.where(own_pipe, total.reshape(4, 32, 128), 0.0), axis=1)

    def at_ends(value):
        spread = jnp.where(own_pipe, value[:, None, :], 0.0).reshape(128, 128)
        return dot(jnp.concatenate(split3(spread), axis=1), insert).reshape(4, 32, 256)

    def block_row(ref, a):
        return end_row(ref[0, a], ref[1, a])

    def apply(blocks, value):
        total = blocks[0] * value[0:1]
        for a in range(1, 4):
            total = total + blocks[a] * value[a : a + 1]
        return total

    for load in loads[2:6]:
        load.wait()
    out_blocks = [block_row(jout, a) for a in range(4)]
    in_blocks = [block_row(jin, a) for a in range(4)]

    def block_ends(blocks, at):
        total = dot(blocks, at).reshape(16, 32, 128)
        total = jnp.sum(jnp.where(own_pipe, total, 0.0), axis=1)
        return [total[4 * a : 4 * a + 4] for a in range(4)]

    pre_blocks = jnp.concatenate([precond[a, b] for b in range(4) for a in range(4)], axis=0)
    pre_ends = block_ends(pre_blocks, extract)
    to_balance = [
        sum(out_blocks[a] * pre_ends[b][a : a + 1] for a in range(4)) for b in range(4)
    ]

    to_table = (slot_of_junction_col == iota((128, 256), 1).astype(F32)).astype(F32).astype(BF16)

    def stacked(value):
        high = value.astype(BF16).astype(F32)
        middle = (value - high).astype(BF16).astype(F32)
        low = value - high - middle
        return jnp.concatenate([high, middle, low, jnp.zeros_like(high)], axis=0).astype(BF16)

    def unstacked(total):
        return total[0:8] + total[8:16] + total[16:24]

    def eight(value):
        return jnp.concatenate([value, jnp.zeros_like(value)], axis=0)

    def fill(sends, balance, free):
        table = unstacked(dot(stacked(eight(balance)), to_table))
        for version in range(4):
            shifted = pltpu.roll(table, 32 * version, 1) if version else table
            sends[version, 0:4] = shifted[0:4, :128]
            sends[version, 4:8] = shifted[0:4, 128:]
            sends[version, 8:12] = pltpu.roll(free, 32, 1) if version % 2 else free

    def post(sends, recvs, near_rows, send_sem, recv_sem):
        copies = []
        for offset in sorted(range(-FAR, FAR + 1), key=lambda o: -abs(o)):
            if offset == 0:
                continue
            count = near_rows if abs(offset) <= SPAN else 8
            copy = pltpu.make_async_remote_copy(
                src_ref=sends.at[-offset % 4, 0:count],
                dst_ref=recvs.at[FAR - offset, 0:count],
                send_sem=send_sem.at[FAR + offset],
                recv_sem=recv_sem.at[FAR + offset],
                device_id=near(offset),
                device_id_type=MESH,
            )
            copy.start()
            copies.append(copy)
        recvs[FAR, 0:near_rows] = sends[0, 0:near_rows]
        return copies

    def pieces(recvs, part):
        joined = []
        for index in range(0, PIECES, 2):
            value = recvs[SPAN + index, part]
            if index + 1 < PIECES:
                value = value + recvs[SPAN + index + 1, part]
            joined.append(value)
        return joined

    def near_balances(recvs, gather):
        starts = []
        for first in range(0, PEERS, 4):
            total = recvs[first, 0:8]
            for index in range(first + 1, min(first + 4, PEERS)):
                total = total + recvs[index, 0:8]
            starts.append(total)
        table = [starts[k + 1] + pltpu.roll(starts[k], 4, 0) for k in range(4)]
        left = stacked(jnp.concatenate(table, axis=1))
        return [
            unstacked(dot(left[:, 128 * (j // 2) : 128 * (j // 2) + 256], gather[j]))[0:4]
            for j in range(5)
        ]

    def next_balances(first, frees, blocks, crosses, matches):
        second = []
        for j in range(5):
            turned = pltpu.roll(first[j], 96, 1)
            cross = apply(crosses[j], turned)
            second.append(frees[j] + apply(blocks[j], first[j]) + pltpu.roll(cross, 96, 1))
        own = dot(stacked(eight(jnp.concatenate(second, axis=1))), matches)
        return unstacked(own)[0:4]

    def advance(source, target, picture=None):
        for first in range(0, 32, CHUNK):
            part = slice(first, first + CHUNK)
            vec = [source[b, part] for b in range(4)]
            x = []
            for a in range(4):
                total = precond[a, 0, part].astype(F32) * vec[0]
                for b in range(1, 4):
                    total = total + precond[a, b, part].astype(F32) * vec[b]
                if picture is not None:
                    picture[a, part] = total
                x.append(total)
            keep = active[part]
            slot = iota((CHUNK, 256), 1)
            for b in range(4):
                sums = []
                for blocks in (diag, lower, upper):
                    total = blocks[0, b, part].astype(F32) * x[0]
                    for a in range(1, 4):
                        total = total + blocks[a, b, part].astype(F32) * x[a]
                    sums.append(total)
                following = jnp.where(slot == 255, 0.0, pltpu.roll(sums[1], 255, 1))
                preceding = jnp.where(slot == 0, 0.0, pltpu.roll(sums[2], 1, 1))
                total = jnp.where(keep, sums[0] + following + preceding, 0.0)
                target[b, part] = total - SHIFT * vec[b]

    def inner(left, right_part):
        total = jnp.sum(left * right_part, axis=(0, 1)).reshape(1, 256)
        return total[:, :128] + total[:, 128:]

    half = (lane & 32) == 0
    pack = []
    for a in range(4):
        turned = pltpu.roll(in_blocks[a], 64, 1)
        own = apply(to_balance, in_blocks[a])
        cross = single * apply(to_balance, turned)
        pack.append(own + pltpu.roll(cross, 32, 1))
    pack = jnp.concatenate(pack, axis=0)
    place_row = jnp.where((lane & 32) == 0, slot_of_junction_row + 1.0, 0.0)
    for version in range(4):
        turn = 32 * (version % 2)
        sends_one[version, 12:13] = pltpu.roll(place_row, turn, 1) if turn else place_row
    block_sends[0] = pack
    block_sends[1] = pltpu.roll(pack, 32, 1)

    start = jnp.where(active[None], right[...], 0.0)
    basis[0] = start
    start_ends = ends_of(start)
    balance = apply(to_balance, start_ends)
    for load in loads[6:]:
        load.wait()
    advance(basis.at[0], bulk, image.at[0])
    bulk_ends = ends_of(bulk[...])
    free = apply(to_balance, bulk_ends)
    fill(sends_one, balance, free)
    pl.semaphore_wait(barrier, len(partners))
    copies = post(sends_one, recvs_one, 13, near_send.at[0], near_recv.at[0])
    block_copies = []
    for offset in sorted(range(-SPAN, SPAN + 1), key=lambda o: -abs(o)):
        if offset != 0:
            copy = pltpu.make_async_remote_copy(
                src_ref=block_sends.at[offset % 2],
                dst_ref=block_recvs.at[SPAN - offset],
                send_sem=block_send.at[SPAN + offset],
                recv_sem=block_recv.at[SPAN + offset],
                device_id=near(offset),
                device_id_type=MESH,
            )
            copy.start()
            block_copies.append(copy)
    block_recvs[SPAN] = block_sends[0]
    pending = copies + block_copies

    advance(bulk, spare.at[0])
    spare_ends = ends_of(spare[0])
    advance(spare.at[0], spare.at[1])
    far_ends = ends_of(spare[1])
    is_first = lane < 64
    used = (lane & 32) == 0
    extracts = [extract]
    for depth in (1, 2):
        slot = jnp.where(is_first, depth, length_row - 1 - depth)
        slot = jnp.where(used & (length_row > depth), slot, -1)
        extracts.append((iota((256, 128), 0) == slot).astype(F32).astype(BF16))
    pre_at = [pre_ends] + [block_ends(pre_blocks, extracts[d]) for d in (1, 2)]
    diag_at = [block_ends(diag[...].reshape(512, 256), extracts[d]) for d in (0, 1)]
    lower_at = [block_ends(lower[...].reshape(512, 256), extracts[d]) for d in range(3)]
    upper_at = [block_ends(upper[...].reshape(512, 256), extracts[d]) for d in range(3)]
    inward = [None] + [
        [jnp.where(is_first, lower_at[d][a], upper_at[d][a]) for a in range(4)] for d in (1, 2)
    ]
    outward = [
        [
            jnp.where(
                length_row > d + 1, jnp.where(is_first, upper_at[d][a], lower_at[d][a]), 0.0
            )
            for a in range(4)
        ]
        for d in (0, 1)
    ]
    of_length = [((length_row == count) & used).astype(F32) for count in (1, 2, 3)]

    def at_depths(added):
        other = pltpu.roll(added, 64, 1)
        return [added + of_length[0] * other, of_length[1] * other, of_length[2] * other]

    def step_at_end(value):
        x = [apply(pre_at[d], value[d]) for d in (0, 1)]
        return apply(diag_at[0], x[0]) + apply(inward[1], x[1]) - SHIFT * value[0]

    def step_at_ends(value):
        x = [apply(pre_at[d], value[d]) for d in range(3)]
        return [
            apply(diag_at[0], x[0]) + apply(inward[1], x[1]) - SHIFT * value[0],
            apply(diag_at[1], x[1])
            + apply(outward[0], x[0])
            + apply(inward[2], x[2])
            - SHIFT * value[1],
        ]

    for copy in copies:
        copy.wait_recv()

    joined = pieces(recvs_one, slice(8, 13))
    gather = []
    place_rows = []
    for j in range(5):
        tagged = joined[j][4:5]
        column = 2.0 * j + jnp.where(half, 0.0, 1.0)
        position = jnp.where(tagged > 0.5, tagged - 1.0 + 32.0 * column, -1000.0)
        place_rows.append(position)
        rows_of = iota((256, 128), 0).astype(F32) + 128.0 * (j // 2)
        gather.append((rows_of == position).astype(F32).astype(BF16))
    own_place = jnp.where(slot_of_junction_col < 0.0, -2000.0, slot_of_junction_col + 128.0)
    matches = (own_place == jnp.concatenate(place_rows, axis=1)).astype(F32).T.astype(BF16)
    first = near_balances(recvs_one, gather)
    for copy in block_copies:
        copy.wait_recv()
    blocks = []
    crosses = []
    for index in range(0, PIECES, 2):
        even = block_recvs[index]
        odd = block_recvs[index + 1] if index + 1 < PIECES else jnp.zeros_like(even)
        own = jnp.where(half, even, odd)
        cross = jnp.where(half, odd, even)
        blocks.append([own[4 * a : 4 * a + 4] for a in range(4)])
        crosses.append([cross[4 * a : 4 * a + 4] for a in range(4)])

    second = next_balances(first, [value[0:4] for value in joined], blocks, crosses, matches)
    added_one = apply(in_blocks, first[2])
    added_two = apply(in_blocks, second)
    moved = step_at_ends(at_depths(added_one))
    moved = [value + more for value, more in zip(moved, at_depths(added_two))]
    ends_at = [
        start_ends,
        bulk_ends + at_depths(added_one)[0],
        spare_ends + moved[0],
        far_ends + step_at_end(moved),
    ]
    balance = apply(to_balance, ends_at[2])
    free = apply(to_balance, ends_at[3])
    fill(sends_two, balance, free)
    copies = post(sends_two, recvs_two, 12, near_send.at[1], near_recv.at[1])
    pending += copies
    basis[1] = bulk[...] + at_ends(added_one)
    advance(basis.at[1], bulk, image.at[1])
    basis[2] = bulk[...] + at_ends(added_two)
    advance(basis.at[2], bulk, image.at[2])

    advance(bulk, spare.at[0])
    vectors = [basis.at[0], basis.at[1], basis.at[2], bulk, spare.at[0]]
    for index, (i, j) in enumerate(PAIRS):
        gram_own[0, index : index + 1] = inner(vectors[i][...], vectors[j][...])
    gram_own[0, len(PAIRS) : GRAM_ROWS] = jnp.zeros((GRAM_ROWS - len(PAIRS), 128), F32)

    def apply_transposed(blocks, value):
        return jnp.concatenate(
            [jnp.sum(block * value, axis=0, keepdims=True) for block in blocks], axis=0
        )

    def step_transposed(value):
        x = apply_transposed(diag_at[0], value[0]) + apply_transposed(outward[0], value[1])
        return apply_transposed(pre_at[0], x) - SHIFT * value[0]

    ends_at.append(ends_of(spare[0]))
    turned_at = [
        step_transposed([value, ends_of(vector[...], extracts[1])])
        for value, vector in zip(ends_at, vectors)
    ]
    for copy in copies:
        copy.wait_recv()

    joined = pieces(recvs_two, slice(8, 12))
    first = near_balances(recvs_two, gather)
    second = next_balances(first, joined, blocks, crosses, matches)
    added_one = apply(in_blocks, first[2])
    added_two = apply(in_blocks, second)
    put_one = at_depths(added_one)
    put_two = at_depths(added_two)
    moved = step_at_ends(put_one)
    more = [ends_at[i] * added_one for i in range(3)]
    more.append((2.0 * ends_at[3] + put_one[0]) * added_one)
    more += [turned_at[i] * added_one + ends_at[i] * added_two for i in range(3)]
    more.append(
        (turned_at[3] + ends_at[4] + moved[0]) * added_one + (ends_at[3] + put_one[0]) * added_two
    )
    more.append(
        (2.0 * turned_at[4] + step_transposed(moved)) * added_one
        + (2.0 * (ends_at[4] + moved[0]) + put_two[0]) * added_two
    )
    more = [jnp.sum(value, axis=0, keepdims=True) for value in more]
    empty = jnp.zeros((1, 128), F32)
    more = [empty] * 6 + more + [empty] * (GRAM_ROWS - len(PAIRS))

    sums = gram_own[0] + jnp.concatenate(more, axis=0)
    partial = jnp.sum(sums, axis=1, keepdims=True)
    eye = iota((GRAM_ROWS, 128), 0) == iota((GRAM_ROWS, 128), 1)
    mine = row * columns + col
    gram_row[0] = jnp.sum(jnp.where(eye, partial, 0.0), axis=0, keepdims=True)
    gram_all[mine] = gram_row[0]
    others = rows * columns - 1

    def tell(index, carry):
        target = index + jnp.where(index >= row * columns, 1, 0)
        pltpu.make_async_remote_copy(
            src_ref=gram_row.at[0],
            dst_ref=gram_all.at[mine],
            send_sem=all_send,
            recv_sem=all_recv,
            device_id=(target // columns, (col + target) % columns),
            device_id_type=MESH,
        ).start()
        return carry

    lax.fori_loop(0, others, tell, 0, unroll=5)
    basis[3] = bulk[...] + at_ends(added_one)
    for a in range(4):
        value = precond[a, 0].astype(F32) * basis[3, 0]
        for b in range(1, 4):
            value = value + precond[a, b].astype(F32) * basis[3, b]
        image[3, a] = value
    received = gram_all.at[0:others]
    pltpu.make_async_copy(received, received, all_recv).wait()
    total = jnp.sum(gram_all[...], axis=0)
    splat = jnp.sum(jnp.where(eye, total, 0.0), axis=1, keepdims=True)
    splat = jnp.broadcast_to(splat, (GRAM_ROWS, 128))
    gram = {
        pair: jnp.broadcast_to(splat[index : index + 1], (8, 128))
        for index, pair in enumerate(PAIRS)
    }
    coeffs = [jnp.broadcast_to(value[0:1], (32, 128)) for value in krylov_coeffs(gram)]
    for a in range(4):
        for lanes in (slice(0, 128), slice(128, 256)):
            value = coeffs[0] * image[0, a, :, lanes]
            for k in range(1, ITERS):
                value = value + coeffs[k] * image[k, a, :, lanes]
            result[a, :, lanes] = value
    for copy in pending:
        copy.wait_send()
    pltpu.make_async_copy(received, received, all_send).wait()


def body(rows, columns, right_side, diag, lower, upper, precond, jout, jin, junction, length):
    pipes, slots = right_side.shape[1:]
    length = length.reshape(1, pipes)
    operands = (right_side, diag, lower, upper, precond, jout, jin, junction, length)
    held = [pltpu.with_memory_space_constraint(value, pltpu.HBM) for value in operands]
    inputs = [pltpu.VMEM(value.shape, value.dtype) for value in operands]
    return pl.pallas_call(
        functools.partial(kernel, rows, columns),
        out_shape=pltpu.VMEM(right_side.shape, F32),
        in_specs=[pl.BlockSpec(memory_space=pltpu.HBM)] * len(operands),
        out_specs=pl.BlockSpec(memory_space=pltpu.VMEM),
        scratch_shapes=inputs
        + [
            pltpu.VMEM((ITERS, 4, pipes, slots), F32),
            pltpu.VMEM((ITERS, 4, pipes, slots), F32),
            pltpu.VMEM((4, pipes, slots), F32),
            pltpu.VMEM((2, 4, pipes, slots), F32),
            pltpu.VMEM((4, 16, 128), F32),
            pltpu.VMEM((4, 16, 128), F32),
            pltpu.VMEM((2, 16, 128), F32),
            pltpu.VMEM((PEERS, 16, 128), F32),
            pltpu.VMEM((PEERS, 16, 128), F32),
            pltpu.VMEM((PIECES, 16, 128), F32),
            pltpu.VMEM((1, GRAM_ROWS, 128), F32),
            pltpu.VMEM((1, 1, 128), F32),
            pltpu.VMEM((rows * columns, 1, 128), F32),
            pltpu.SemaphoreType.DMA((len(operands),)),
            pltpu.SemaphoreType.DMA((2, PEERS)),
            pltpu.SemaphoreType.DMA((2, PEERS)),
            pltpu.SemaphoreType.DMA((PIECES,)),
            pltpu.SemaphoreType.DMA((PIECES,)),
            pltpu.SemaphoreType.DMA,
            pltpu.SemaphoreType.DMA,
        ],
        compiler_params=pltpu.CompilerParams(
            collective_id=0, has_side_effects=True, vmem_limit_bytes=48 * 1024 * 1024
        ),
    )(*held)


def solution(mesh):
    in_specs = (
        P(None, ("row", "col"), None),
        P(None, None, ("row", "col"), None),
        P(None, None, ("row", "col"), None),
        P(None, None, ("row", "col"), None),
        P(None, None, ("row", "col"), None),
        P(None, None, None, ("row", "col")),
        P(None, None, None, ("row", "col")),
        P(None, ("row", "col")),
        P(("row", "col")),
    )
    out_specs = P(None, ("row", "col"), None)
    run = functools.partial(body, mesh.shape["row"], mesh.shape["col"])
    return jax.shard_map(run, mesh=mesh, in_specs=in_specs, out_specs=out_specs, check_vma=False)
```

```python
import functools

import jax
import jax.numpy as jnp
from jax import lax
from jax.experimental import pallas as pl
from jax.experimental.pallas import tpu as pltpu
from jax.sharding import PartitionSpec as P

ITERS = 4
REACH = 2
SPAN = 2 * REACH
FAR = 2 * SPAN
PIECES = 2 * SPAN + 1
PEERS = 2 * FAR + 1
SHIFT = 1.0
CHUNK = 16
MESH = pl.DeviceIdType.MESH
F32 = jnp.float32
BF16 = jnp.bfloat16


def iota(shape, dim):
    return lax.broadcasted_iota(jnp.int32, shape, dim)


def split3(value):
    high = value.astype(BF16)
    rest = value - high.astype(F32)
    middle = rest.astype(BF16)
    low = (rest - middle.astype(F32)).astype(BF16)
    return high, middle, low


def dot(a, b):
    return lax.dot_general(a, b, (((1,), (0,)), ((), ())), preferred_element_type=F32)


def end_row(first, last):
    empty = jnp.zeros_like(first)
    return jnp.concatenate([first, empty, last, empty], axis=1)


def least_squares(hess, beta, steps):
    upper = [list(line) for line in hess]
    target = [beta] + [None] * steps
    cosines = []
    sines = []
    inverses = []
    for k in range(steps):
        for i in range(k):
            temp = cosines[i] * upper[i][k] + sines[i] * upper[i + 1][k]
            upper[i + 1][k] = cosines[i] * upper[i + 1][k] - sines[i] * upper[i][k]
            upper[i][k] = temp
        inverse = lax.rsqrt(upper[k][k] * upper[k][k] + upper[k + 1][k] * upper[k + 1][k])
        cosines.append(upper[k][k] * inverse)
        sines.append(upper[k + 1][k] * inverse)
        inverses.append(inverse)
        target[k + 1] = -sines[k] * target[k]
        target[k] = cosines[k] * target[k]
    coeffs = [None] * steps
    for k in range(steps - 1, -1, -1):
        total = target[k]
        for j in range(k + 1, steps):
            total = total - upper[k][j] * coeffs[j]
        coeffs[k] = total * inverses[k]
    return coeffs


def krylov_coeffs(gram):
    size = ITERS + 1
    low = [[None] * size for _ in range(size)]
    for j in range(size):
        total = gram[j, j]
        for k in range(j):
            total = total - low[j][k] * low[j][k]
        total = jnp.maximum(total, 1e-7 * gram[j, j])
        inverse = lax.rsqrt(total)
        low[j][j] = total * inverse
        for i in range(j + 1, size):
            total = gram[j, i]
            for k in range(j):
                total = total - low[i][k] * low[j][k]
            low[i][j] = total * inverse
    hess = [[None] * ITERS for _ in range(size)]
    for k in range(ITERS):
        for i in range(k + 2):
            hess[i][k] = low[k + 1][i]
            if i <= k:
                hess[i][k] = hess[i][k] + SHIFT * low[k][i]
    return least_squares(hess, low[0][0], ITERS)


PAIRS = [(i, j) for j in range(ITERS + 1) for i in range(j + 1)]
GRAM_ROWS = 16


def kernel(
    rows,
    columns,
    right_hbm,
    diag_hbm,
    lower_hbm,
    upper_hbm,
    precond_hbm,
    out_hbm_blocks,
    in_hbm_blocks,
    junction_hbm,
    length_hbm,
    result,
    right,
    diag,
    lower,
    upper,
    precond,
    jout,
    jin,
    junction,
    length,
    basis,
    image,
    bulk,
    spare,
    sends_one,
    sends_two,
    block_sends,
    recvs_one,
    recvs_two,
    block_recvs,
    gram_own,
    gram_row,
    gram_all,
    in_sems,
    near_send,
    near_recv,
    block_send,
    block_recv,
    all_send,
    all_recv,
):
    row = lax.axis_index("row")
    col = lax.axis_index("col")

    def near(offset):
        return (row, (col + offset + columns) % columns)

    barrier = pltpu.get_barrier_semaphore()
    partners = [near(offset) for offset in range(-FAR, FAR + 1) if offset != 0]
    partners += [((row + step) % rows, col) for step in range(1, rows)]
    for partner in partners:
        pl.semaphore_signal(barrier, inc=1, device_id=partner, device_id_type=MESH)

    loads = [
        pltpu.make_async_copy(source, target, in_sems.at[index])
        for index, (source, target) in enumerate(
            [
                (length_hbm, length),
                (junction_hbm, junction),
                (out_hbm_blocks, jout),
                (in_hbm_blocks, jin),
                (right_hbm, right),
                (precond_hbm, precond),
                (diag_hbm, diag),
                (lower_hbm, lower),
                (upper_hbm, upper),
            ]
        )
    ]
    for load in loads:
        load.start()

    sends_one[...] = jnp.zeros_like(sends_one)
    sends_two[...] = jnp.zeros_like(sends_two)
    for load in loads[:2]:
        load.wait()

    lane = iota((1, 128), 1)
    lengths = length[...]
    length_row = end_row(lengths, lengths)
    slot_row = jnp.where(
        (lane & 32) != 0, -1, end_row(jnp.zeros_like(lengths), lengths - 1)
    )
    extract = (iota((256, 128), 0) == slot_row).astype(F32).astype(BF16)
    ids = junction[...]
    owned = ids % 32
    ids = (ids // 32 - col + REACH + columns) % columns * 32 + owned
    slot_of_junction_row = jnp.where((lane & 32) != 0, -1, end_row(ids[0:1], ids[1:2])).astype(F32)
    square = iota((128, 128), 0) == iota((128, 128), 1)
    slot_col = jnp.sum(jnp.where(square, slot_row.astype(F32), 0.0), axis=1, keepdims=True)
    slot_of_junction_col = jnp.sum(
        jnp.where(square, slot_of_junction_row, 0.0), axis=1, keepdims=True
    )
    insert = (iota((128, 256), 1).astype(F32) == slot_col).astype(F32)
    insert = jnp.concatenate([insert] * 3, axis=0).astype(BF16)
    length_col = jnp.sum(
        jnp.where(square[:32], length_row.astype(F32), 0.0), axis=1, keepdims=True
    )
    active = iota((32, 256), 1).astype(F32) < length_col
    single = ((length_row == 1) & ((lane & 32) == 0)).astype(F32)
    own_pipe = (iota((32, 128), 0) == (iota((32, 128), 1) & 63))[None]

    def ends_of(value, at=extract):
        total = sum(dot(part, at) for part in split3(value.reshape(128, 256)))
        return jnp.sum(jnp.where(own_pipe, total.reshape(4, 32, 128), 0.0), axis=1)

    def at_ends(value):
        spread = jnp.where(own_pipe, value[:, None, :], 0.0).reshape(128, 128)
        return dot(jnp.concatenate(split3(spread), axis=1), insert).reshape(4, 32, 256)

    def block_row(ref, a):
        return end_row(ref[0, a], ref[1, a])

    def apply(blocks, value):
        total = blocks[0] * value[0:1]
        for a in range(1, 4):
            total = total + blocks[a] * value[a : a + 1]
        return total

    for load in loads[2:6]:
        load.wait()
    out_blocks = [block_row(jout, a) for a in range(4)]
    in_blocks = [block_row(jin, a) for a in range(4)]

    def block_ends(blocks, at):
        total = dot(blocks, at).reshape(16, 32, 128)
        total = jnp.sum(jnp.where(own_pipe, total, 0.0), axis=1)
        return [total[4 * a : 4 * a + 4] for a in range(4)]

    pre_blocks = jnp.concatenate([precond[a, b] for b in range(4) for a in range(4)], axis=0)
    pre_ends = block_ends(pre_blocks, extract)
    to_balance = [
        sum(out_blocks[a] * pre_ends[b][a : a + 1] for a in range(4)) for b in range(4)
    ]

    to_table = (slot_of_junction_col == iota((128, 256), 1).astype(F32)).astype(F32).astype(BF16)

    def stacked(value):
        high = value.astype(BF16).astype(F32)
        middle = (value - high).astype(BF16).astype(F32)
        low = value - high - middle
        return jnp.concatenate([high, middle, low, jnp.zeros_like(high)], axis=0).astype(BF16)

    def unstacked(total):
        return total[0:8] + total[8:16] + total[16:24]

    def eight(value):
        return jnp.concatenate([value, jnp.zeros_like(value)], axis=0)

    def fill(sends, balance, free):
        table = unstacked(dot(stacked(eight(balance)), to_table))
        for version in range(4):
            shifted = pltpu.roll(table, 32 * version, 1) if version else table
            sends[version, 0:4] = shifted[0:4, :128]
            sends[version, 4:8] = shifted[0:4, 128:]
            sends[version, 8:12] = pltpu.roll(free, 32, 1) if version % 2 else free

    def post(sends, recvs, near_rows, send_sem, recv_sem):
        copies = []
        for offset in sorted(range(-FAR, FAR + 1), key=lambda o: -abs(o)):
            if offset == 0:
                continue
            count = near_rows if abs(offset) <= SPAN else 8
            copy = pltpu.make_async_remote_copy(
                src_ref=sends.at[-offset % 4, 0:count],
                dst_ref=recvs.at[FAR - offset, 0:count],
                send_sem=send_sem.at[FAR + offset],
                recv_sem=recv_sem.at[FAR + offset],
                device_id=near(offset),
                device_id_type=MESH,
            )
            copy.start()
            copies.append(copy)
        recvs[FAR, 0:near_rows] = sends[0, 0:near_rows]
        return copies

    def pieces(recvs, part):
        joined = []
        for index in range(0, PIECES, 2):
            value = recvs[SPAN + index, part]
            if index + 1 < PIECES:
                value = value + recvs[SPAN + index + 1, part]
            joined.append(value)
        return joined

    def near_balances(recvs, gather):
        starts = []
        for first in range(0, PEERS, 4):
            total = recvs[first, 0:8]
            for index in range(first + 1, min(first + 4, PEERS)):
                total = total + recvs[index, 0:8]
            starts.append(total)
        table = [starts[k + 1] + pltpu.roll(starts[k], 4, 0) for k in range(4)]
        left = stacked(jnp.concatenate(table, axis=1))
        return [
            unstacked(dot(left[:, 128 * (j // 2) : 128 * (j // 2) + 256], gather[j]))[0:4]
            for j in range(5)
        ]

    def next_balances(first, frees, blocks, crosses, matches):
        second = []
        for j in range(5):
            turned = pltpu.roll(first[j], 96, 1)
            cross = apply(crosses[j], turned)
            second.append(frees[j] + apply(blocks[j], first[j]) + pltpu.roll(cross, 96, 1))
        own = dot(stacked(eight(jnp.concatenate(second, axis=1))), matches)
        return unstacked(own)[0:4]

    def advance(source, target, picture=None):
        for first in range(0, 32, CHUNK):
            part = slice(first, first + CHUNK)
            vec = [source[b, part] for b in range(4)]
            x = []
            for a in range(4):
                total = precond[a, 0, part].astype(F32) * vec[0]
                for b in range(1, 4):
                    total = total + precond[a, b, part].astype(F32) * vec[b]
                if picture is not None:
                    picture[a, part] = total
                x.append(total)
            keep = active[part]
            slot = iota((CHUNK, 256), 1)
            for b in range(4):
                sums = []
                for blocks in (diag, lower, upper):
                    total = blocks[0, b, part].astype(F32) * x[0]
                    for a in range(1, 4):
                        total = total + blocks[a, b, part].astype(F32) * x[a]
                    sums.append(total)
                following = jnp.where(slot == 255, 0.0, pltpu.roll(sums[1], 255, 1))
                preceding = jnp.where(slot == 0, 0.0, pltpu.roll(sums[2], 1, 1))
                total = jnp.where(keep, sums[0] + following + preceding, 0.0)
                target[b, part] = total - SHIFT * vec[b]

    def inner(left, right_part):
        total = jnp.sum(left * right_part, axis=(0, 1)).reshape(1, 256)
        return total[:, :128] + total[:, 128:]

    half = (lane & 32) == 0
    pack = []
    for a in range(4):
        turned = pltpu.roll(in_blocks[a], 64, 1)
        own = apply(to_balance, in_blocks[a])
        cross = single * apply(to_balance, turned)
        pack.append(own + pltpu.roll(cross, 32, 1))
    pack = jnp.concatenate(pack, axis=0)
    place_row = jnp.where((lane & 32) == 0, slot_of_junction_row + 1.0, 0.0)
    for version in range(4):
        turn = 32 * (version % 2)
        sends_one[version, 12:13] = pltpu.roll(place_row, turn, 1) if turn else place_row
    block_sends[0] = pack
    block_sends[1] = pltpu.roll(pack, 32, 1)

    start = jnp.where(active[None], right[...], 0.0)
    basis[0] = start
    start_ends = ends_of(start)
    balance = apply(to_balance, start_ends)
    for load in loads[6:]:
        load.wait()
    advance(basis.at[0], bulk, image.at[0])
    bulk_ends = ends_of(bulk[...])
    free = apply(to_balance, bulk_ends)
    fill(sends_one, balance, free)
    pl.semaphore_wait(barrier, len(partners))
    copies = post(sends_one, recvs_one, 13, near_send.at[0], near_recv.at[0])
    block_copies = []
    for offset in sorted(range(-SPAN, SPAN + 1), key=lambda o: -abs(o)):
        if offset != 0:
            copy = pltpu.make_async_remote_copy(
                src_ref=block_sends.at[offset % 2],
                dst_ref=block_recvs.at[SPAN - offset],
                send_sem=block_send.at[SPAN + offset],
                recv_sem=block_recv.at[SPAN + offset],
                device_id=near(offset),
                device_id_type=MESH,
            )
            copy.start()
            block_copies.append(copy)
    block_recvs[SPAN] = block_sends[0]
    pending = copies + block_copies

    advance(bulk, spare.at[0])
    spare_ends = ends_of(spare[0])
    advance(spare.at[0], spare.at[1])
    far_ends = ends_of(spare[1])
    is_first = lane < 64
    used = (lane & 32) == 0
    extracts = [extract]
    for depth in (1, 2):
        slot = jnp.where(is_first, depth, length_row - 1 - depth)
        slot = jnp.where(used & (length_row > depth), slot, -1)
        extracts.append((iota((256, 128), 0) == slot).astype(F32).astype(BF16))
    pre_at = [pre_ends] + [block_ends(pre_blocks, extracts[d]) for d in (1, 2)]
    diag_at = [block_ends(diag[...].reshape(512, 256), extracts[d]) for d in (0, 1)]
    lower_at = [block_ends(lower[...].reshape(512, 256), extracts[d]) for d in range(3)]
    upper_at = [block_ends(upper[...].reshape(512, 256), extracts[d]) for d in range(3)]
    inward = [None] + [
        [jnp.where(is_first, lower_at[d][a], upper_at[d][a]) for a in range(4)] for d in (1, 2)
    ]
    outward = [
        [
            jnp.where(
                length_row > d + 1, jnp.where(is_first, upper_at[d][a], lower_at[d][a]), 0.0
            )
            for a in range(4)
        ]
        for d in (0, 1)
    ]
    of_length = [((length_row == count) & used).astype(F32) for count in (1, 2, 3)]

    def at_depths(added):
        other = pltpu.roll(added, 64, 1)
        return [added + of_length[0] * other, of_length[1] * other, of_length[2] * other]

    def step_at_end(value):
        x = [apply(pre_at[d], value[d]) for d in (0, 1)]
        return apply(diag_at[0], x[0]) + apply(inward[1], x[1]) - SHIFT * value[0]

    def step_at_ends(value):
        x = [apply(pre_at[d], value[d]) for d in range(3)]
        return [
            apply(diag_at[0], x[0]) + apply(inward[1], x[1]) - SHIFT * value[0],
            apply(diag_at[1], x[1])
            + apply(outward[0], x[0])
            + apply(inward[2], x[2])
            - SHIFT * value[1],
        ]

    for copy in copies:
        copy.wait_recv()

    joined = pieces(recvs_one, slice(8, 13))
    gather = []
    place_rows = []
    for j in range(5):
        tagged = joined[j][4:5]
        column = 2.0 * j + jnp.where(half, 0.0, 1.0)
        position = jnp.where(tagged > 0.5, tagged - 1.0 + 32.0 * column, -1000.0)
        place_rows.append(position)
        rows_of = iota((256, 128), 0).astype(F32) + 128.0 * (j // 2)
        gather.append((rows_of == position).astype(F32).astype(BF16))
    own_place = jnp.where(slot_of_junction_col < 0.0, -2000.0, slot_of_junction_col + 128.0)
    matches = (own_place == jnp.concatenate(place_rows, axis=1)).astype(F32).T.astype(BF16)
    first = near_balances(recvs_one, gather)
    for copy in block_copies:
        copy.wait_recv()
    blocks = []
    crosses = []
    for index in range(0, PIECES, 2):
        even = block_recvs[index]
        odd = block_recvs[index + 1] if index + 1 < PIECES else jnp.zeros_like(even)
        own = jnp.where(half, even, odd)
        cross = jnp.where(half, odd, even)
        blocks.append([own[4 * a : 4 * a + 4] for a in range(4)])
        crosses.append([cross[4 * a : 4 * a + 4] for a in range(4)])

    second = next_balances(first, [value[0:4] for value in joined], blocks, crosses, matches)
    added_one = apply(in_blocks, first[2])
    added_two = apply(in_blocks, second)
    moved = step_at_ends(at_depths(added_one))
    moved = [value + more for value, more in zip(moved, at_depths(added_two))]
    ends_at = [
        start_ends,
        bulk_ends + at_depths(added_one)[0],
        spare_ends + moved[0],
        far_ends + step_at_end(moved),
    ]
    balance = apply(to_balance, ends_at[2])
    free = apply(to_balance, ends_at[3])
    fill(sends_two, balance, free)
    copies = post(sends_two, recvs_two, 12, near_send.at[1], near_recv.at[1])
    pending += copies
    basis[1] = bulk[...] + at_ends(added_one)
    advance(basis.at[1], bulk, image.at[1])
    basis[2] = bulk[...] + at_ends(added_two)
    advance(basis.at[2], bulk, image.at[2])

    advance(bulk, spare.at[0])
    vectors = [basis.at[0], basis.at[1], basis.at[2], bulk, spare.at[0]]
    for index, (i, j) in enumerate(PAIRS):
        gram_own[0, index : index + 1] = inner(vectors[i][...], vectors[j][...])
    gram_own[0, len(PAIRS) : GRAM_ROWS] = jnp.zeros((GRAM_ROWS - len(PAIRS), 128), F32)

    def apply_transposed(blocks, value):
        return jnp.concatenate(
            [jnp.sum(block * value, axis=0, keepdims=True) for block in blocks], axis=0
        )

    def step_transposed(value):
        x = apply_transposed(diag_at[0], value[0]) + apply_transposed(outward[0], value[1])
        return apply_transposed(pre_at[0], x) - SHIFT * value[0]

    ends_at.append(ends_of(spare[0]))
    turned_at = [
        step_transposed([value, ends_of(vector[...], extracts[1])])
        for value, vector in zip(ends_at, vectors)
    ]
    for copy in copies:
        copy.wait_recv()

    joined = pieces(recvs_two, slice(8, 12))
    first = near_balances(recvs_two, gather)
    second = next_balances(first, joined, blocks, crosses, matches)
    added_one = apply(in_blocks, first[2])
    added_two = apply(in_blocks, second)
    put_one = at_depths(added_one)
    put_two = at_depths(added_two)
    moved = step_at_ends(put_one)
    more = [ends_at[i] * added_one for i in range(3)]
    more.append((2.0 * ends_at[3] + put_one[0]) * added_one)
    more += [turned_at[i] * added_one + ends_at[i] * added_two for i in range(3)]
    more.append(
        (turned_at[3] + ends_at[4] + moved[0]) * added_one + (ends_at[3] + put_one[0]) * added_two
    )
    more.append(
        (2.0 * turned_at[4] + step_transposed(moved)) * added_one
        + (2.0 * (ends_at[4] + moved[0]) + put_two[0]) * added_two
    )
    more = [jnp.sum(value, axis=0, keepdims=True) for value in more]
    empty = jnp.zeros((1, 128), F32)
    more = [empty] * 6 + more + [empty] * (GRAM_ROWS - len(PAIRS))

    sums = gram_own[0] + jnp.concatenate(more, axis=0)
    partial = jnp.sum(sums, axis=1, keepdims=True)
    eye = iota((GRAM_ROWS, 128), 0) == iota((GRAM_ROWS, 128), 1)
    mine = row * columns + col
    gram_row[0] = jnp.sum(jnp.where(eye, partial, 0.0), axis=0, keepdims=True)
    gram_all[pl.ds(mine, 1)] = gram_row[0]
    others = rows * columns - 1

    def tell(index, carry):
        target = index + jnp.where(index >= row * columns, 1, 0)
        pltpu.make_async_remote_copy(
            src_ref=gram_row.at[0],
            dst_ref=gram_all.at[pl.ds(mine, 1)],
            send_sem=all_send,
            recv_sem=all_recv,
            device_id=(target // columns, (col + target) % columns),
            device_id_type=MESH,
        ).start()
        return carry

    lax.fori_loop(0, others, tell, 0, unroll=5)
    basis[3] = bulk[...] + at_ends(added_one)
    for a in range(4):
        value = precond[a, 0].astype(F32) * basis[3, 0]
        for b in range(1, 4):
            value = value + precond[a, b].astype(F32) * basis[3, b]
        image[3, a] = value
    received = gram_all.at[0:others]
    for copy in pending:
        copy.wait_send()
    pltpu.make_async_copy(received, received, all_send).wait()
    pltpu.make_async_copy(received, received, all_recv).wait()
    total = jnp.sum(gram_all[...], axis=0, keepdims=True)
    splat = jnp.sum(jnp.where(eye, total, 0.0), axis=1, keepdims=True)
    splat = jnp.broadcast_to(splat, (GRAM_ROWS, 128))
    gram = {
        pair: jnp.broadcast_to(splat[index : index + 1], (8, 128))
        for index, pair in enumerate(PAIRS)
    }
    coeffs = [jnp.broadcast_to(value[0:1], (32, 128)) for value in krylov_coeffs(gram)]
    for a in range(4):
        for lanes in (slice(0, 128), slice(128, 256)):
            value = coeffs[0] * image[0, a, :, lanes]
            for k in range(1, ITERS):
                value = value + coeffs[k] * image[k, a, :, lanes]
            result[a, :, lanes] = value


def body(rows, columns, right_side, diag, lower, upper, precond, jout, jin, junction, length):
    pipes, slots = right_side.shape[1:]
    length = length.reshape(1, pipes)
    operands = (right_side, diag, lower, upper, precond, jout, jin, junction, length)
    held = [pltpu.with_memory_space_constraint(value, pltpu.HBM) for value in operands]
    inputs = [pltpu.VMEM(value.shape, value.dtype) for value in operands]
    return pl.pallas_call(
        functools.partial(kernel, rows, columns),
        out_shape=pltpu.VMEM(right_side.shape, F32),
        in_specs=[pl.BlockSpec(memory_space=pltpu.HBM)] * len(operands),
        out_specs=pl.BlockSpec(memory_space=pltpu.VMEM),
        scratch_shapes=inputs
        + [
            pltpu.VMEM((ITERS, 4, pipes, slots), F32),
            pltpu.VMEM((ITERS, 4, pipes, slots), F32),
            pltpu.VMEM((4, pipes, slots), F32),
            pltpu.VMEM((2, 4, pipes, slots), F32),
            pltpu.VMEM((4, 16, 128), F32),
            pltpu.VMEM((4, 16, 128), F32),
            pltpu.VMEM((2, 16, 128), F32),
            pltpu.VMEM((PEERS, 16, 128), F32),
            pltpu.VMEM((PEERS, 16, 128), F32),
            pltpu.VMEM((PIECES, 16, 128), F32),
            pltpu.VMEM((1, GRAM_ROWS, 128), F32),
            pltpu.VMEM((1, 1, 128), F32),
            pltpu.VMEM((rows * columns, 128), F32),
            pltpu.SemaphoreType.DMA((len(operands),)),
            pltpu.SemaphoreType.DMA((2, PEERS)),
            pltpu.SemaphoreType.DMA((2, PEERS)),
            pltpu.SemaphoreType.DMA((PIECES,)),
            pltpu.SemaphoreType.DMA((PIECES,)),
            pltpu.SemaphoreType.DMA,
            pltpu.SemaphoreType.DMA,
        ],
        compiler_params=pltpu.CompilerParams(
            collective_id=0, has_side_effects=True, vmem_limit_bytes=48 * 1024 * 1024
        ),
    )(*held)


def solution(mesh):
    in_specs = (
        P(None, ("row", "col"), None),
        P(None, None, ("row", "col"), None),
        P(None, None, ("row", "col"), None),
        P(None, None, ("row", "col"), None),
        P(None, None, ("row", "col"), None),
        P(None, None, None, ("row", "col")),
        P(None, None, None, ("row", "col")),
        P(None, ("row", "col")),
        P(("row", "col")),
    )
    out_specs = P(None, ("row", "col"), None)
    run = functools.partial(body, mesh.shape["row"], mesh.shape["col"])
    return jax.shard_map(run, mesh=mesh, in_specs=in_specs, out_specs=out_specs, check_vma=False)
```

```python
import functools

import jax
import jax.numpy as jnp
from jax import lax
from jax.experimental import pallas as pl
from jax.experimental.pallas import tpu as pltpu
from jax.sharding import PartitionSpec as P

ITERS = 4
REACH = 2
SPAN = 2 * REACH
FAR = 2 * SPAN
PIECES = 2 * SPAN + 1
PEERS = 2 * FAR + 1
SCALE = 0.0625
SHIFT = SCALE
CHUNK = 16
MESH = pl.DeviceIdType.MESH
F32 = jnp.float32
BF16 = jnp.bfloat16


def iota(shape, dim):
    return lax.broadcasted_iota(jnp.int32, shape, dim)


def split3(value):
    high = value.astype(BF16)
    rest = value - high.astype(F32)
    middle = rest.astype(BF16)
    low = (rest - middle.astype(F32)).astype(BF16)
    return high, middle, low


def dot(a, b):
    return lax.dot_general(a, b, (((1,), (0,)), ((), ())), preferred_element_type=F32)


def end_row(first, last):
    empty = jnp.zeros_like(first)
    return jnp.concatenate([first, empty, last, empty], axis=1)


def least_squares(hess, beta, steps):
    upper = [list(line) for line in hess]
    target = [beta] + [None] * steps
    cosines = []
    sines = []
    inverses = []
    for k in range(steps):
        for i in range(k):
            temp = cosines[i] * upper[i][k] + sines[i] * upper[i + 1][k]
            upper[i + 1][k] = cosines[i] * upper[i + 1][k] - sines[i] * upper[i][k]
            upper[i][k] = temp
        inverse = lax.rsqrt(upper[k][k] * upper[k][k] + upper[k + 1][k] * upper[k + 1][k])
        cosines.append(upper[k][k] * inverse)
        sines.append(upper[k + 1][k] * inverse)
        inverses.append(inverse)
        target[k + 1] = -sines[k] * target[k]
        target[k] = cosines[k] * target[k]
    coeffs = [None] * steps
    for k in range(steps - 1, -1, -1):
        total = target[k]
        for j in range(k + 1, steps):
            total = total - upper[k][j] * coeffs[j]
        coeffs[k] = total * inverses[k]
    return coeffs


def krylov_coeffs(gram):
    size = ITERS + 1
    low = [[None] * size for _ in range(size)]
    for j in range(size):
        total = gram[j, j]
        for k in range(j):
            total = total - low[j][k] * low[j][k]
        total = jnp.maximum(total, 1e-7 * gram[j, j])
        inverse = lax.rsqrt(total)
        low[j][j] = total * inverse
        for i in range(j + 1, size):
            total = gram[j, i]
            for k in range(j):
                total = total - low[i][k] * low[j][k]
            low[i][j] = total * inverse
    hess = [[None] * ITERS for _ in range(size)]
    for k in range(ITERS):
        for i in range(k + 2):
            hess[i][k] = low[k + 1][i]
            if i <= k:
                hess[i][k] = hess[i][k] + SHIFT * low[k][i]
    return least_squares(hess, low[0][0], ITERS)


PAIRS = [(i, j) for j in range(ITERS + 1) for i in range(j + 1)]
GRAM_ROWS = 16


def kernel(
    rows,
    columns,
    right_hbm,
    diag_hbm,
    lower_hbm,
    upper_hbm,
    precond_hbm,
    out_hbm_blocks,
    in_hbm_blocks,
    junction_hbm,
    length_hbm,
    result,
    right,
    diag,
    lower,
    upper,
    precond,
    jout,
    jin,
    junction,
    length,
    basis,
    image,
    bulk,
    spare,
    sends_one,
    sends_two,
    block_sends,
    recvs_one,
    recvs_two,
    block_recvs,
    gram_own,
    gram_row,
    gram_all,
    in_sems,
    near_send,
    near_recv,
    block_send,
    block_recv,
    all_send,
    all_recv,
):
    row = lax.axis_index("row")
    col = lax.axis_index("col")

    def near(offset):
        return (row, (col + offset + columns) % columns)

    barrier = pltpu.get_barrier_semaphore()
    partners = [near(offset) for offset in range(-FAR, FAR + 1) if offset != 0]
    partners += [((row + step) % rows, col) for step in range(1, rows)]
    for partner in partners:
        pl.semaphore_signal(barrier, inc=1, device_id=partner, device_id_type=MESH)

    loads = [
        pltpu.make_async_copy(source, target, in_sems.at[index])
        for index, (source, target) in enumerate(
            [
                (length_hbm, length),
                (junction_hbm, junction),
                (out_hbm_blocks, jout),
                (in_hbm_blocks, jin),
                (right_hbm, right),
                (precond_hbm, precond),
                (diag_hbm, diag),
                (lower_hbm, lower),
                (upper_hbm, upper),
            ]
        )
    ]
    for load in loads:
        load.start()

    sends_one[...] = jnp.zeros_like(sends_one)
    sends_two[...] = jnp.zeros_like(sends_two)
    for load in loads[:2]:
        load.wait()

    lane = iota((1, 128), 1)
    lengths = length[...]
    length_row = end_row(lengths, lengths)
    slot_row = jnp.where(
        (lane & 32) != 0, -1, end_row(jnp.zeros_like(lengths), lengths - 1)
    )
    extract = (iota((256, 128), 0) == slot_row).astype(F32).astype(BF16)
    ids = junction[...]
    owned = ids % 32
    ids = (ids // 32 - col + REACH + columns) % columns * 32 + owned
    slot_of_junction_row = jnp.where((lane & 32) != 0, -1, end_row(ids[0:1], ids[1:2])).astype(F32)
    square = iota((128, 128), 0) == iota((128, 128), 1)
    slot_col = jnp.sum(jnp.where(square, slot_row.astype(F32), 0.0), axis=1, keepdims=True)
    slot_of_junction_col = jnp.sum(
        jnp.where(square, slot_of_junction_row, 0.0), axis=1, keepdims=True
    )
    insert = (iota((128, 256), 1).astype(F32) == slot_col).astype(F32)
    insert = jnp.concatenate([insert] * 3, axis=0).astype(BF16)
    length_col = jnp.sum(
        jnp.where(square[:32], length_row.astype(F32), 0.0), axis=1, keepdims=True
    )
    active = iota((32, 256), 1).astype(F32) < length_col
    single = ((length_row == 1) & ((lane & 32) == 0)).astype(F32)
    own_pipe = (iota((32, 128), 0) == (iota((32, 128), 1) & 63))[None]

    def ends_of(value, at=extract):
        total = sum(dot(part, at) for part in split3(value.reshape(128, 256)))
        return jnp.sum(jnp.where(own_pipe, total.reshape(4, 32, 128), 0.0), axis=1)

    def at_ends(value):
        spread = jnp.where(own_pipe, value[:, None, :], 0.0).reshape(128, 128)
        return dot(jnp.concatenate(split3(spread), axis=1), insert).reshape(4, 32, 256)

    def block_row(ref, a):
        return end_row(ref[0, a], ref[1, a])

    def apply(blocks, value):
        total = blocks[0] * value[0:1]
        for a in range(1, 4):
            total = total + blocks[a] * value[a : a + 1]
        return total

    for load in loads[2:6]:
        load.wait()
    out_blocks = [block_row(jout, a) for a in range(4)]
    in_blocks = [block_row(jin, a) for a in range(4)]

    def block_ends(blocks, at):
        total = dot(blocks, at).reshape(16, 32, 128)
        total = jnp.sum(jnp.where(own_pipe, total, 0.0), axis=1)
        return [total[4 * a : 4 * a + 4] for a in range(4)]

    pre_blocks = jnp.concatenate([precond[a, b] for b in range(4) for a in range(4)], axis=0)
    pre_ends = [SCALE * value for value in block_ends(pre_blocks, extract)]
    to_balance = [
        sum(out_blocks[a] * pre_ends[b][a : a + 1] for a in range(4)) for b in range(4)
    ]

    to_table = (slot_of_junction_col == iota((128, 256), 1).astype(F32)).astype(F32).astype(BF16)

    def stacked(value):
        high = value.astype(BF16).astype(F32)
        middle = (value - high).astype(BF16).astype(F32)
        low = value - high - middle
        return jnp.concatenate([high, middle, low, jnp.zeros_like(high)], axis=0).astype(BF16)

    def unstacked(total):
        return total[0:8] + total[8:16] + total[16:24]

    def eight(value):
        return jnp.concatenate([value, jnp.zeros_like(value)], axis=0)

    def fill(sends, balance, free):
        table = unstacked(dot(stacked(eight(balance)), to_table))
        for version in range(4):
            shifted = pltpu.roll(table, 32 * version, 1) if version else table
            sends[version, 0:4] = shifted[0:4, :128]
            sends[version, 4:8] = shifted[0:4, 128:]
            sends[version, 8:12] = pltpu.roll(free, 32, 1) if version % 2 else free

    def post(sends, recvs, near_rows, send_sem, recv_sem):
        copies = []
        for offset in sorted(range(-FAR, FAR + 1), key=lambda o: -abs(o)):
            if offset == 0:
                continue
            count = near_rows if abs(offset) <= SPAN else 8
            copy = pltpu.make_async_remote_copy(
                src_ref=sends.at[-offset % 4, 0:count],
                dst_ref=recvs.at[FAR - offset, 0:count],
                send_sem=send_sem.at[FAR + offset],
                recv_sem=recv_sem.at[FAR + offset],
                device_id=near(offset),
                device_id_type=MESH,
            )
            copy.start()
            copies.append(copy)
        recvs[FAR, 0:near_rows] = sends[0, 0:near_rows]
        return copies

    def pieces(recvs, part):
        joined = []
        for index in range(0, PIECES, 2):
            value = recvs[SPAN + index, part]
            if index + 1 < PIECES:
                value = value + recvs[SPAN + index + 1, part]
            joined.append(value)
        return joined

    def near_balances(recvs, gather):
        starts = []
        for first in range(0, PEERS, 4):
            total = recvs[first, 0:8]
            for index in range(first + 1, min(first + 4, PEERS)):
                total = total + recvs[index, 0:8]
            starts.append(total)
        table = [starts[k + 1] + pltpu.roll(starts[k], 4, 0) for k in range(4)]
        left = stacked(jnp.concatenate(table, axis=1))
        return [
            unstacked(dot(left[:, 128 * (j // 2) : 128 * (j // 2) + 256], gather[j]))[0:4]
            for j in range(5)
        ]

    def next_balances(first, frees, blocks, crosses, matches):
        second = []
        for j in range(5):
            turned = pltpu.roll(first[j], 96, 1)
            cross = apply(crosses[j], turned)
            second.append(frees[j] + apply(blocks[j], first[j]) + pltpu.roll(cross, 96, 1))
        own = dot(stacked(eight(jnp.concatenate(second, axis=1))), matches)
        return unstacked(own)[0:4]

    def advance(source, target, picture=None):
        for first in range(0, 32, CHUNK):
            part = slice(first, first + CHUNK)
            vec = [source[b, part] for b in range(4)]
            x = []
            for a in range(4):
                total = precond[a, 0, part].astype(F32) * vec[0]
                for b in range(1, 4):
                    total = total + precond[a, b, part].astype(F32) * vec[b]
                total = SCALE * total
                if picture is not None:
                    picture[a, part] = total
                x.append(total)
            keep = active[part]
            slot = iota((CHUNK, 256), 1)
            for b in range(4):
                sums = []
                for blocks in (diag, lower, upper):
                    total = blocks[0, b, part].astype(F32) * x[0]
                    for a in range(1, 4):
                        total = total + blocks[a, b, part].astype(F32) * x[a]
                    sums.append(total)
                following = jnp.where(slot == 255, 0.0, pltpu.roll(sums[1], 255, 1))
                preceding = jnp.where(slot == 0, 0.0, pltpu.roll(sums[2], 1, 1))
                total = jnp.where(keep, sums[0] + following + preceding, 0.0)
                target[b, part] = total - SHIFT * vec[b]

    def inner(left, right_part):
        total = jnp.sum(left * right_part, axis=(0, 1)).reshape(1, 256)
        return total[:, :128] + total[:, 128:]

    half = (lane & 32) == 0
    pack = []
    for a in range(4):
        turned = pltpu.roll(in_blocks[a], 64, 1)
        own = apply(to_balance, in_blocks[a])
        cross = single * apply(to_balance, turned)
        pack.append(own + pltpu.roll(cross, 32, 1))
    pack = jnp.concatenate(pack, axis=0)
    place_row = jnp.where((lane & 32) == 0, slot_of_junction_row + 1.0, 0.0)
    for version in range(4):
        turn = 32 * (version % 2)
        sends_one[version, 12:13] = pltpu.roll(place_row, turn, 1) if turn else place_row
    block_sends[0] = pack
    block_sends[1] = pltpu.roll(pack, 32, 1)

    start = jnp.where(active[None], right[...], 0.0)
    basis[0] = start
    start_ends = ends_of(start)
    balance = apply(to_balance, start_ends)
    for load in loads[6:]:
        load.wait()
    advance(basis.at[0], bulk, image.at[0])
    bulk_ends = ends_of(bulk[...])
    free = apply(to_balance, bulk_ends)
    fill(sends_one, balance, free)
    pl.semaphore_wait(barrier, len(partners))
    copies = post(sends_one, recvs_one, 13, near_send.at[0], near_recv.at[0])
    block_copies = []
    for offset in sorted(range(-SPAN, SPAN + 1), key=lambda o: -abs(o)):
        if offset != 0:
            copy = pltpu.make_async_remote_copy(
                src_ref=block_sends.at[offset % 2],
                dst_ref=block_recvs.at[SPAN - offset],
                send_sem=block_send.at[SPAN + offset],
                recv_sem=block_recv.at[SPAN + offset],
                device_id=near(offset),
                device_id_type=MESH,
            )
            copy.start()
            block_copies.append(copy)
    block_recvs[SPAN] = block_sends[0]
    pending = copies + block_copies

    advance(bulk, spare.at[0])
    spare_ends = ends_of(spare[0])
    advance(spare.at[0], spare.at[1])
    far_ends = ends_of(spare[1])
    is_first = lane < 64
    used = (lane & 32) == 0
    extracts = [extract]
    for depth in (1, 2):
        slot = jnp.where(is_first, depth, length_row - 1 - depth)
        slot = jnp.where(used & (length_row > depth), slot, -1)
        extracts.append((iota((256, 128), 0) == slot).astype(F32).astype(BF16))
    pre_at = [pre_ends] + [
        [SCALE * value for value in block_ends(pre_blocks, extracts[d])] for d in (1, 2)
    ]
    diag_at = [block_ends(diag[...].reshape(512, 256), extracts[d]) for d in (0, 1)]
    lower_at = [block_ends(lower[...].reshape(512, 256), extracts[d]) for d in range(3)]
    upper_at = [block_ends(upper[...].reshape(512, 256), extracts[d]) for d in range(3)]
    inward = [None] + [
        [jnp.where(is_first, lower_at[d][a], upper_at[d][a]) for a in range(4)] for d in (1, 2)
    ]
    outward = [
        [
            jnp.where(
                length_row > d + 1, jnp.where(is_first, upper_at[d][a], lower_at[d][a]), 0.0
            )
            for a in range(4)
        ]
        for d in (0, 1)
    ]
    of_length = [((length_row == count) & used).astype(F32) for count in (1, 2, 3)]

    def at_depths(added):
        other = pltpu.roll(added, 64, 1)
        return [added + of_length[0] * other, of_length[1] * other, of_length[2] * other]

    def step_at_end(value):
        x = [apply(pre_at[d], value[d]) for d in (0, 1)]
        return apply(diag_at[0], x[0]) + apply(inward[1], x[1]) - SHIFT * value[0]

    def step_at_ends(value):
        x = [apply(pre_at[d], value[d]) for d in range(3)]
        return [
            apply(diag_at[0], x[0]) + apply(inward[1], x[1]) - SHIFT * value[0],
            apply(diag_at[1], x[1])
            + apply(outward[0], x[0])
            + apply(inward[2], x[2])
            - SHIFT * value[1],
        ]

    for copy in copies:
        copy.wait_recv()

    joined = pieces(recvs_one, slice(8, 13))
    gather = []
    place_rows = []
    for j in range(5):
        tagged = joined[j][4:5]
        column = 2.0 * j + jnp.where(half, 0.0, 1.0)
        position = jnp.where(tagged > 0.5, tagged - 1.0 + 32.0 * column, -1000.0)
        place_rows.append(position)
        rows_of = iota((256, 128), 0).astype(F32) + 128.0 * (j // 2)
        gather.append((rows_of == position).astype(F32).astype(BF16))
    own_place = jnp.where(slot_of_junction_col < 0.0, -2000.0, slot_of_junction_col + 128.0)
    matches = (own_place == jnp.concatenate(place_rows, axis=1)).astype(F32).T.astype(BF16)
    first = near_balances(recvs_one, gather)
    for copy in block_copies:
        copy.wait_recv()
    blocks = []
    crosses = []
    for index in range(0, PIECES, 2):
        even = block_recvs[index]
        odd = block_recvs[index + 1] if index + 1 < PIECES else jnp.zeros_like(even)
        own = jnp.where(half, even, odd)
        cross = jnp.where(half, odd, even)
        blocks.append([own[4 * a : 4 * a + 4] for a in range(4)])
        crosses.append([cross[4 * a : 4 * a + 4] for a in range(4)])

    second = next_balances(first, [value[0:4] for value in joined], blocks, crosses, matches)
    added_one = apply(in_blocks, first[2])
    added_two = apply(in_blocks, second)
    moved = step_at_ends(at_depths(added_one))
    moved = [value + more for value, more in zip(moved, at_depths(added_two))]
    ends_at = [
        start_ends,
        bulk_ends + at_depths(added_one)[0],
        spare_ends + moved[0],
        far_ends + step_at_end(moved),
    ]
    balance = apply(to_balance, ends_at[2])
    free = apply(to_balance, ends_at[3])
    fill(sends_two, balance, free)
    copies = post(sends_two, recvs_two, 12, near_send.at[1], near_recv.at[1])
    pending += copies
    basis[1] = bulk[...] + at_ends(added_one)
    advance(basis.at[1], bulk, image.at[1])
    basis[2] = bulk[...] + at_ends(added_two)
    advance(basis.at[2], bulk, image.at[2])

    advance(bulk, spare.at[0])
    vectors = [basis.at[0], basis.at[1], basis.at[2], bulk, spare.at[0]]
    for index, (i, j) in enumerate(PAIRS):
        gram_own[0, index : index + 1] = inner(vectors[i][...], vectors[j][...])
    gram_own[0, len(PAIRS) : GRAM_ROWS] = jnp.zeros((GRAM_ROWS - len(PAIRS), 128), F32)

    def apply_transposed(blocks, value):
        return jnp.concatenate(
            [jnp.sum(block * value, axis=0, keepdims=True) for block in blocks], axis=0
        )

    def step_transposed(value):
        x = apply_transposed(diag_at[0], value[0]) + apply_transposed(outward[0], value[1])
        return apply_transposed(pre_at[0], x) - SHIFT * value[0]

    ends_at.append(ends_of(spare[0]))
    turned_at = [
        step_transposed([value, ends_of(vector[...], extracts[1])])
        for value, vector in zip(ends_at, vectors)
    ]
    for copy in copies:
        copy.wait_recv()

    joined = pieces(recvs_two, slice(8, 12))
    first = near_balances(recvs_two, gather)
    second = next_balances(first, joined, blocks, crosses, matches)
    added_one = apply(in_blocks, first[2])
    added_two = apply(in_blocks, second)
    put_one = at_depths(added_one)
    put_two = at_depths(added_two)
    moved = step_at_ends(put_one)
    more = [ends_at[i] * added_one for i in range(3)]
    more.append((2.0 * ends_at[3] + put_one[0]) * added_one)
    more += [turned_at[i] * added_one + ends_at[i] * added_two for i in range(3)]
    more.append(
        (turned_at[3] + ends_at[4] + moved[0]) * added_one + (ends_at[3] + put_one[0]) * added_two
    )
    more.append(
        (2.0 * turned_at[4] + step_transposed(moved)) * added_one
        + (2.0 * (ends_at[4] + moved[0]) + put_two[0]) * added_two
    )
    more = [jnp.sum(value, axis=0, keepdims=True) for value in more]
    empty = jnp.zeros((1, 128), F32)
    more = [empty] * 6 + more + [empty] * (GRAM_ROWS - len(PAIRS))

    sums = gram_own[0] + jnp.concatenate(more, axis=0)
    partial = jnp.sum(sums, axis=1, keepdims=True)
    eye = iota((GRAM_ROWS, 128), 0) == iota((GRAM_ROWS, 128), 1)
    mine = row * columns + col
    gram_row[0] = jnp.sum(jnp.where(eye, partial, 0.0), axis=0, keepdims=True)
    gram_all[pl.ds(mine, 1)] = gram_row[0]
    others = rows * columns - 1

    def tell(index, carry):
        target = index + jnp.where(index >= row * columns, 1, 0)
        pltpu.make_async_remote_copy(
            src_ref=gram_row.at[0],
            dst_ref=gram_all.at[pl.ds(mine, 1)],
            send_sem=all_send,
            recv_sem=all_recv,
            device_id=(target // columns, (col + target) % columns),
            device_id_type=MESH,
        ).start()
        return carry

    lax.fori_loop(0, others, tell, 0, unroll=5)
    basis[3] = bulk[...] + at_ends(added_one)
    for a in range(4):
        value = precond[a, 0].astype(F32) * basis[3, 0]
        for b in range(1, 4):
            value = value + precond[a, b].astype(F32) * basis[3, b]
        image[3, a] = SCALE * value
    received = gram_all.at[0:others]
    for copy in pending:
        copy.wait_send()
    pltpu.make_async_copy(received, received, all_send).wait()
    pltpu.make_async_copy(received, received, all_recv).wait()
    total = jnp.sum(gram_all[...], axis=0, keepdims=True)
    splat = jnp.sum(jnp.where(eye, total, 0.0), axis=1, keepdims=True)
    splat = jnp.broadcast_to(splat, (GRAM_ROWS, 128))
    gram = {
        pair: jnp.broadcast_to(splat[index : index + 1], (8, 128))
        for index, pair in enumerate(PAIRS)
    }
    coeffs = [jnp.broadcast_to(value[0:1], (32, 128)) for value in krylov_coeffs(gram)]
    for a in range(4):
        for lanes in (slice(0, 128), slice(128, 256)):
            value = coeffs[0] * image[0, a, :, lanes]
            for k in range(1, ITERS):
                value = value + coeffs[k] * image[k, a, :, lanes]
            result[a, :, lanes] = value


def body(rows, columns, right_side, diag, lower, upper, precond, jout, jin, junction, length):
    pipes, slots = right_side.shape[1:]
    length = length.reshape(1, pipes)
    operands = (right_side, diag, lower, upper, precond, jout, jin, junction, length)
    held = [pltpu.with_memory_space_constraint(value, pltpu.HBM) for value in operands]
    inputs = [pltpu.VMEM(value.shape, value.dtype) for value in operands]
    return pl.pallas_call(
        functools.partial(kernel, rows, columns),
        out_shape=pltpu.VMEM(right_side.shape, F32),
        in_specs=[pl.BlockSpec(memory_space=pltpu.HBM)] * len(operands),
        out_specs=pl.BlockSpec(memory_space=pltpu.VMEM),
        scratch_shapes=inputs
        + [
            pltpu.VMEM((ITERS, 4, pipes, slots), F32),
            pltpu.VMEM((ITERS, 4, pipes, slots), F32),
            pltpu.VMEM((4, pipes, slots), F32),
            pltpu.VMEM((2, 4, pipes, slots), F32),
            pltpu.VMEM((4, 16, 128), F32),
            pltpu.VMEM((4, 16, 128), F32),
            pltpu.VMEM((2, 16, 128), F32),
            pltpu.VMEM((PEERS, 16, 128), F32),
            pltpu.VMEM((PEERS, 16, 128), F32),
            pltpu.VMEM((PIECES, 16, 128), F32),
            pltpu.VMEM((1, GRAM_ROWS, 128), F32),
            pltpu.VMEM((1, 1, 128), F32),
            pltpu.VMEM((rows * columns, 128), F32),
            pltpu.SemaphoreType.DMA((len(operands),)),
            pltpu.SemaphoreType.DMA((2, PEERS)),
            pltpu.SemaphoreType.DMA((2, PEERS)),
            pltpu.SemaphoreType.DMA((PIECES,)),
            pltpu.SemaphoreType.DMA((PIECES,)),
            pltpu.SemaphoreType.DMA,
            pltpu.SemaphoreType.DMA,
        ],
        compiler_params=pltpu.CompilerParams(
            collective_id=0, has_side_effects=True, vmem_limit_bytes=48 * 1024 * 1024
        ),
    )(*held)


def solution(mesh):
    in_specs = (
        P(None, ("row", "col"), None),
        P(None, None, ("row", "col"), None),
        P(None, None, ("row", "col"), None),
        P(None, None, ("row", "col"), None),
        P(None, None, ("row", "col"), None),
        P(None, None, None, ("row", "col")),
        P(None, None, None, ("row", "col")),
        P(None, ("row", "col")),
        P(("row", "col")),
    )
    out_specs = P(None, ("row", "col"), None)
    run = functools.partial(body, mesh.shape["row"], mesh.shape["col"])
    return jax.shard_map(run, mesh=mesh, in_specs=in_specs, out_specs=out_specs, check_vma=False)
```
